512 devices in a mesh: cfg: 2 (over core), seq: 128 (over y_lo, z, x), tile: 2 (over y_hi).
Axes of the slice: x: 4, y: 8 (y_hi: 2, y_lo: 4; y = y_hi * 4 + y_lo), z: 8, core: 2. Of those that a mesh axis runs over, the one named last changes fastest.
Arguments:
- section_input: bfloat16 [4, 128, 1024, 384], P('tile', None, 'seq'), may hold values from -6 to 6
- norm_gain: float32 [384], replicated, may hold values from 0.5 to 1.5
- conv_weight: bfloat16 [384, 864], replicated, may hold values from -0.0625 to 0.0625
- conv_bias: float32 [32], replicated, may hold values from -3 to 3
- mean_weight: float32 [32, 16], replicated, may hold values from -1 to 1
- mean_bias: float32 [16], replicated, may hold values from -3 to 3
- noisy_tokens: bfloat16 [131072, 64], P(('seq', 'tile')), may hold values from -6 to 6
- mask_tokens: bfloat16 [131072, 128], P(('seq', 'tile')), may hold values from 0 to 1
- patch_weight: bfloat16 [64, 5120], replicated, may hold values from -0.75 to 0.75
- patch_bias: float32 [5120], replicated, may hold values from -3 to 3
- context_weight: bfloat16 [192, 5120], replicated, may hold values from -0.4375 to 0.4375
- context_bias: float32 [5120], replicated, may hold values from -3 to 3
- norm_shift: float32 [5120], replicated, may hold values from -3 to 3
- norm_scale: float32 [5120], replicated, may hold values from -3 to 3
Outputs:
- block_input: bfloat16 [131072, 5120], P(('seq', 'tile'))
The draws below stay inside these ranges and needn't reach their ends.
All inputs are finite; a program needn't handle non-finite values.
Results may differ from the reference program's by a relative error of at most 0.004.
Values may be sent and summed in bfloat16 or wider, within the bound.
No kernel may reach another device: no remote copies, remote signals or barrier semaphores. Data moves between devices by JAX's collectives and lax.ppermute only.
A program may use at most 128 MiB of HBM per device.

```python
import jax
import jax.numpy as jnp
from jax import lax

D = 5120
C = 384
Z = 16
MC = 32
K = 3
H = 128
ZO = 32
F = 4
W = 1024
S = 131072
N_SEQ = 128
N_TILE = 2


def block_scale(rng, shape, shards, least, top_value):
    loudness, own = 1.0, jax.random.fold_in(rng, 6)
    for axis_at, shards_of in shards:
        draws = jnp.exp(jax.random.uniform(jax.random.fold_in(own, axis_at), (shards_of,), jnp.float32, least / len(shards), top_value / len(shards)))
        loudness = loudness * jnp.repeat(draws, shape[axis_at] // shards_of).reshape([-1 if axis == axis_at else 1 for axis in range(len(shape))])
    return loudness


def noise(key, shape, scale, most, split=(), dtype=jnp.bfloat16):
    entries = scale * jax.random.normal(key, shape, jnp.float32)
    if split:
        entries = entries * block_scale(key, shape, split, -0.22, 0.18)
    return jnp.clip(entries, -most, most).astype(dtype)


def setup_inputs(seed: int = 0) -> dict:
    key_of = jax.random.split(jax.random.key(seed), 15)
    return {
        "section_input": noise(key_of[0], (F, H, W, C), 1.0, 6.0, ((0, 2), (2, 128))),
        "norm_gain": jnp.clip(jax.random.uniform(key_of[1], (C,), jnp.float32, 0.5, 1.5), 0.5, 1.5),
        "conv_weight": noise(key_of[2], (C, K * K * K * ZO), (K * K * K * C) ** -0.5, 0.0625),
        "conv_bias": noise(key_of[3], (ZO,), 0.5, 3.0, (), jnp.float32),
        "mean_weight": noise(key_of[4], (ZO, Z), ZO ** -0.5, 1.0, (), jnp.float32),
        "mean_bias": noise(key_of[5], (Z,), 0.5, 3.0, (), jnp.float32),
        "noisy_tokens": noise(key_of[6], (S, 4 * Z), 1.0, 6.0, ((0, 256),)),
        "mask_tokens": jnp.clip(1.0 * jax.random.uniform(key_of[7], (S, 4 * MC), jnp.float32) ** block_scale(key_of[7], (S, 4 * MC), ((0, 256),), -0.2, 0.2), 0.0, 1.0).astype(jnp.bfloat16),
        "patch_weight": noise(key_of[8], (4 * Z, D), (4 * Z) ** -0.5, 0.75),
        "patch_bias": noise(key_of[9], (D,), 0.5, 3.0, (), jnp.float32),
        "context_weight": noise(key_of[10], (4 * Z + 4 * MC, D), (4 * Z + 4 * MC) ** -0.5, 0.4375),
        "context_bias": noise(key_of[11], (D,), 0.5, 3.0, (), jnp.float32),
        "norm_shift": noise(key_of[12], (D,), 0.5, 3.0, (), jnp.float32),
        "norm_scale": noise(key_of[13], (D,), 0.5, 3.0, (), jnp.float32),
    }


def reference(section_input, norm_gain, conv_weight, conv_bias, mean_weight, mean_bias, noisy_tokens, mask_tokens, patch_weight, patch_bias, context_weight, context_bias, norm_shift, norm_scale):
    frames, height, columns, channels = section_input.shape
    values = section_input.astype(jnp.float32)
    energy = lax.optimization_barrier(jnp.mean(values * values, axis=-1, keepdims=True))
    activation = jax.nn.silu(values * lax.rsqrt(energy + 1e-06) * norm_gain).astype(jnp.bfloat16)
    padded = jnp.pad(activation, ((2, 0), (1, 1), (1, 1), (0, 0)))
    kernel = conv_weight.reshape(channels, K, K, K, -1)
    out_chans = kernel.shape[-1]
    convolved = jnp.zeros((frames * height * columns, out_chans), jnp.float32)
    for step_t in range(K):
        for step_h in range(K):
            for step_w in range(K):
                window = padded[step_t:step_t + frames, step_h:step_h + height, step_w:step_w + columns]
                convolved = convolved + jnp.dot(window.reshape(-1, channels), kernel[:, step_t, step_h, step_w], preferred_element_type=jnp.float32)
    convolved = convolved + conv_bias
    latent = (jnp.dot(convolved, mean_weight, precision=lax.Precision.HIGHEST) + mean_bias).astype(jnp.bfloat16)
    latent_dim = latent.shape[-1]
    latent = latent.reshape(frames, height // 2, 2, columns // 2, 2, latent_dim)
    latent_tokens = latent.transpose(0, 1, 3, 5, 2, 4).reshape(-1, 4 * latent_dim)
    blocks = N_SEQ * N_TILE
    split_at = 4 * latent_dim

    def embed_block(pieces):
        own_latent, own_noise, own_mask = pieces
        main_part = jnp.dot(own_noise, patch_weight, preferred_element_type=jnp.float32) + patch_bias
        context_part = jnp.dot(own_latent, context_weight[:split_at], preferred_element_type=jnp.float32)
        context_part = context_part + jnp.dot(own_mask, context_weight[split_at:], preferred_element_type=jnp.float32) + context_bias
        combined = main_part + context_part
        centred = combined - lax.optimization_barrier(jnp.mean(combined, axis=-1, keepdims=True))
        variance = lax.optimization_barrier(jnp.mean(centred * centred, axis=-1, keepdims=True))
        return (centred * lax.rsqrt(variance + 1e-06) * (1.0 + norm_scale) + norm_shift).astype(jnp.bfloat16)
    result = lax.map(embed_block, (latent_tokens.reshape(blocks, -1, split_at), noisy_tokens.reshape(blocks, -1, noisy_tokens.shape[-1]), mask_tokens.reshape(blocks, -1, mask_tokens.shape[-1])))
    return result.reshape(-1, result.shape[-1])
```

```python
import jax
import jax.numpy as jnp
from jax import lax
from jax.experimental import pallas as pl
from jax.experimental.pallas import tpu as pltpu
from jax.sharding import PartitionSpec as P

BF = jnp.bfloat16
F32 = jnp.float32
NT = (((1,), (1,)), ((), ()))


def iota(shape, dim):
    return lax.broadcasted_iota(jnp.int32, shape, dim)


def dot(a, b):
    return jnp.dot(a, b, preferred_element_type=F32)


def dot_nt(a, b):
    return lax.dot_general(a, b, NT, preferred_element_type=F32)


def halves(x):
    high = x.astype(BF)
    return high, (x - high.astype(F32)).astype(BF)


SLOTS = ((0, 2), (0, 1), (1, 2), (1, 1), (0, 0), (0, 2), (1, 0), (1, 2))


def encode_kernel(tile_ref, x_ref, gain_ref, wt_ref, mwt_ref, out_ref, act, big, parts):
    frames, height, columns, channels = x_ref.shape
    pairs = height // 2
    rows = frames * columns
    z, o = mwt_ref.shape
    taps = wt_ref.shape[0] // o
    pick = (iota((o, taps * o), 1) % o == iota((o, taps * o), 0)).astype(BF)
    own = iota((taps * z, taps * o), 0) // z == iota((taps * z, taps * o), 1) // o
    folded = None
    for part in halves(mwt_ref[...]):
        spread = dot(part, pick)
        block = jnp.where(own, jnp.concatenate([spread] * taps, 0), 0.0).astype(BF)
        term = dot(block, wt_ref[...])
        folded = term if folded is None else folded + term
    folded = folded.astype(BF)
    nothing = jnp.zeros((z, channels), BF)
    for t in range(3):
        for slot, (a, e) in enumerate(SLOTS):
            at = (t * 8 + slot) * z
            for k in range(4):
                b = k - a
                tap = ((t * 3 + b) * 3 + e) * z
                value = folded[tap : tap + z] if 0 <= b < 3 else nothing
                big[at : at + z, k * channels : (k + 1) * channels] = value

    zero = jnp.zeros((rows, channels), BF)
    act[0, :, :channels] = zero
    act[pairs, :, channels:] = zero
    step = 8
    gain = gain_ref[...].reshape(1, 1, 1, channels)

    @pl.loop(0, pairs // step)
    def _(j):
        x = x_ref[:, pl.ds(j * 2 * step, 2 * step)].astype(F32)
        energy = jnp.mean(x * x, axis=-1, keepdims=True)
        v = x * lax.rsqrt(energy + 1e-6) * gain
        v = v * (0.5 + 0.5 * jnp.tanh(0.5 * v))
        v = jnp.concatenate([v[f] for f in range(frames)], axis=1).astype(BF)
        v = v.reshape(step, 2, rows, channels)
        act[pl.ds(j * step, step), :, channels:] = v[:, 0]
        act[pl.ds(j * step + 1, step), :, :channels] = v[:, 1]

    first = tile_ref[0] == 0
    lanes = 8 * z
    chunk = 16
    for c in range(pairs // chunk):
        low = act[c * chunk : (c + 1) * chunk].reshape(chunk * rows, 2 * channels)
        high = act[c * chunk + 1 : (c + 1) * chunk + 1].reshape(chunk * rows, 2 * channels)
        out = dot_nt(low, big[:, : 2 * channels]) + dot_nt(high, big[:, 2 * channels :])
        out = out.reshape(chunk // 2, 2, frames, columns, 3 * lanes)
        part = lambda p, f, t: out[:, p, f, :, t * lanes : (t + 1) * lanes]
        for p in range(2):
            ext = (
                part(p, 0, 2),
                part(p, 0, 1) + part(p, 1, 2),
                part(p, 0, 0) + part(p, 1, 1),
                part(p, 1, 0),
            )
            slots = (
                jnp.where(first, ext[0], 0.0),
                jnp.where(first, ext[1], 0.0),
                jnp.where(first, ext[2], ext[0]),
                jnp.where(first, ext[3], ext[1]),
            )
            for f in range(4):
                at = ((p * 4 + f) * (pairs // 2) + c * chunk // 2) * columns
                size = chunk // 2 * columns
                parts[at : at + size] = slots[f].reshape(size, lanes)

    total = parts.shape[0]
    even = parts[pl.ds(0, total // 2, stride=2)]
    odd = parts[pl.ds(1, total // 2, stride=2)]
    slot = iota((1, lanes), 1) // z
    near = pltpu.roll(even, lanes - z, 1)
    far = pltpu.roll(even, lanes - 3 * z, 1)
    moved = jnp.where((slot == 0) | (slot == 2), near, jnp.where((slot == 1) | (slot == 3), far, 0.0))
    back = (slot == 5) | (slot == 7)
    out_ref[...] = jnp.where(back, even, moved + odd).astype(BF)


def prep_kernel(
    ctx_ref, patch_ref, pb_ref, cb_ref, shift_ref, scale_ref, noisy_ref, mask_ref, conv_bias_ref, mwt_ref, mb_ref,
    w_ref, vec_ref, gram_ref, aux_ref, base_ref,
):
    lat = 4 * mwt_ref.shape[0]
    z = lat // 4
    width = ctx_ref.shape[1]
    row, col = iota((lat, lat), 0), iota((lat, lat), 1)
    order = (col == (row % z) * 4 + row // z).astype(BF)
    w_ref[:lat] = dot(order, ctx_ref[:lat]).astype(BF)
    w_ref[lat : 2 * lat] = patch_ref[...]
    w_ref[2 * lat :] = ctx_ref[lat:]
    bias = pb_ref[...] + cb_ref[...]
    mean_b = jnp.mean(bias, axis=1, keepdims=True)
    centred = bias - mean_b
    vec_ref[0:1] = bias
    vec_ref[1:2] = 1.0 + scale_ref[...]
    vec_ref[2:3] = shift_ref[...]
    vec_ref[3:8] = jnp.zeros((5, width), F32)
    w = w_ref[...]
    high, low = halves(centred)
    rows = jnp.concatenate([jnp.ones((1, width), BF), high, low, jnp.zeros((5, width), BF)], 0)
    sums = dot_nt(rows, w)
    mean_w = sums[0:1] / width
    ones = jnp.ones((128, width), BF)
    mean_col = dot_nt(w, ones)[:, :1] / width
    gram = dot_nt(w, w) / width - mean_col * mean_w
    high, low = halves(gram)
    gram_ref[:, : gram.shape[1]] = high
    gram_ref[:, gram.shape[1] :] = low
    size = w.shape[0]
    square = jnp.mean(centred * centred, axis=1, keepdims=True)
    tiled = jnp.concatenate([mwt_ref[...]] * 8, 0)
    conv_bias = jnp.broadcast_to(conv_bias_ref[...], (8, conv_bias_ref.shape[1]))
    latent_bias = lax.dot_general(conv_bias, tiled, NT, precision=lax.Precision.HIGHEST, preferred_element_type=F32)
    latent_bias = latent_bias[:1] + jnp.concatenate([mb_ref[...]] * 8, 1)
    aux_ref[0:1] = mean_w
    aux_ref[1:2] = 2.0 * (sums[1:2] + sums[2:3]) / width
    aux_ref[2:3] = jnp.broadcast_to(mean_b, (1, size))
    aux_ref[3:4] = jnp.broadcast_to(square, (1, size))
    aux_ref[4:5] = jnp.concatenate([latent_bias] * (size // latent_bias.shape[1]), 1)
    aux_ref[5:8] = jnp.zeros((3, size), F32)
    place = (iota((lat, 2 * lat), 1) == iota((lat, 2 * lat), 0) + lat).astype(BF)
    noisy = lax.dot_general(noisy_ref[...], place, (((0,), (0,)), ((), ())), preferred_element_type=F32)
    base_ref[:, : 2 * lat] = noisy.astype(BF)
    base_ref[:, 2 * lat :] = mask_ref[...]


def embed_kernel(arrived_ref, base_ref, w_ref, vec_ref, gram_ref, aux_ref, out_ref, lhs, inv, off):
    @pl.when(pl.program_id(0) == 0)
    def _():
        tokens = base_ref.shape[0]
        lanes = arrived_ref.shape[1]
        z = lanes // 8
        both = arrived_ref[:tokens].astype(F32) + arrived_ref[tokens:].astype(F32)
        crossed = pltpu.roll(both, lanes // 2, 1)
        row = iota((tokens, 1), 0)
        down = jnp.where(row == 0, 0.0, pltpu.roll(crossed, 1, 0))
        up = jnp.where(row == tokens - 1, 0.0, pltpu.roll(crossed, tokens - 1, 0))
        lane = iota((1, lanes), 1)
        latent = both + jnp.where(lane // z % 2 == 0, down, up) + aux_ref[4:5, :lanes]
        front = jnp.where(lane < lanes // 2, latent, base_ref[:, :lanes].astype(F32))
        x = jnp.concatenate([front.astype(BF), base_ref[:, lanes:]], 1)
        lhs[...] = x
        size = x.shape[1]
        y = dot(x, gram_ref[:, :size]) + dot(x, gram_ref[:, size:])
        xf = x.astype(F32)
        mean = jnp.sum(xf * aux_ref[0:1], axis=1, keepdims=True) + aux_ref[2:3, :128]
        variance = jnp.sum((y + aux_ref[1:2]) * xf, axis=1, keepdims=True) + aux_ref[3:4, :128]
        scale = lax.rsqrt(jnp.maximum(variance, 0.0) + 1e-6)
        inv[...] = scale
        off[...] = mean * scale

    combined = dot(lhs[...], w_ref[...]) + vec_ref[0:1]
    copies = combined.shape[1] // inv.shape[1]
    scale = jnp.concatenate([inv[...]] * copies, 1)
    offset = jnp.concatenate([off[...]] * copies, 1)
    out_ref[...] = ((combined * scale - offset) * vec_ref[1:2] + vec_ref[2:3]).astype(BF)


def body(
    section_input, norm_gain, conv_weight, conv_bias, mean_weight, mean_bias, noisy_tokens, mask_tokens,
    patch_weight, patch_bias, context_weight, context_bias, norm_shift, norm_scale,
):
    frames, height, columns, channels = section_input.shape
    z = mean_weight.shape[1]
    tokens = noisy_tokens.shape[0]
    width = patch_weight.shape[1]
    features = patch_weight.shape[0] + context_weight.shape[0]
    shards = lax.axis_size("tile") * lax.axis_size("seq")
    tile = lax.axis_index("tile").astype(jnp.int32).reshape(1)
    vmem = pl.BlockSpec(memory_space=pltpu.VMEM)
    params = pltpu.CompilerParams(vmem_limit_bytes=48 * 1024 * 1024)
    row = lambda v: v.reshape(1, -1)
    message = pl.pallas_call(
        encode_kernel,
        out_shape=jax.ShapeDtypeStruct((shards * 4, 8 * z), BF),
        in_specs=[pl.BlockSpec(memory_space=pltpu.SMEM)] + [vmem] * 4,
        out_specs=vmem,
        scratch_shapes=[
            pltpu.VMEM((height // 2 + 1, frames * columns, 2 * channels), BF),
            pltpu.VMEM((3 * 8 * z, 4 * channels), BF),
            pltpu.VMEM((shards * 8, 8 * z), F32),
        ],
        compiler_params=params,
        name="encode",
    )(tile, section_input, row(norm_gain), conv_weight.T, mean_weight.T)
    arrived = lax.all_to_all(message.reshape(shards, 4, 8 * z), ("tile", "seq"), 0, 0)
    arrived = arrived.reshape(shards * 4, 8 * z)
    weights, vectors, gram, aux, base = pl.pallas_call(
        prep_kernel,
        out_shape=(
            jax.ShapeDtypeStruct((features, width), BF),
            jax.ShapeDtypeStruct((8, width), F32),
            jax.ShapeDtypeStruct((features, 2 * features), BF),
            jax.ShapeDtypeStruct((8, features), F32),
            jax.ShapeDtypeStruct((tokens, features), BF),
        ),
        in_specs=[vmem] * 11,
        out_specs=(vmem,) * 5,
        compiler_params=params,
        cost_estimate=pl.CostEstimate(flops=2 * features * features * width, bytes_accessed=6_000_000, transcendentals=0),
        name="prep",
    )(
        context_weight, patch_weight, row(patch_bias), row(context_bias), row(norm_shift), row(norm_scale),
        noisy_tokens.T, mask_tokens, row(conv_bias), mean_weight.T, row(mean_bias),
    )
    block = 1024
    return pl.pallas_call(
        embed_kernel,
        grid=(width // block,),
        out_shape=jax.ShapeDtypeStruct((tokens, width), BF),
        in_specs=[
            vmem,
            vmem,
            pl.BlockSpec((features, block), lambda n: (0, n)),
            pl.BlockSpec((8, block), lambda n: (0, n)),
            vmem,
            vmem,
        ],
        out_specs=pl.BlockSpec((tokens, block), lambda n: (0, n)),
        scratch_shapes=[
            pltpu.VMEM((tokens, features), BF),
            pltpu.VMEM((tokens, 128), F32),
            pltpu.VMEM((tokens, 128), F32),
        ],
        compiler_params=params,
        name="embed",
    )(arrived, base, weights, vectors, gram, aux)


def solution(mesh):
    placed = (
        P("tile", None, "seq", None),
        P(),
        P(),
        P(),
        P(),
        P(),
        P(("seq", "tile"), None),
        P(("seq", "tile"), None),
        P(),
        P(),
        P(),
        P(),
        P(),
        P(),
    )
    return jax.shard_map(
        body, mesh=mesh, in_specs=placed, out_specs=P(("seq", "tile"), None), check_vma=False
    )
```

```python
import jax
import jax.numpy as jnp
from jax import lax
from jax.experimental import pallas as pl
from jax.experimental.pallas import tpu as pltpu
from jax.sharding import PartitionSpec as P

BF = jnp.bfloat16
F32 = jnp.float32
NT = (((1,), (1,)), ((), ()))


def iota(shape, dim):
    return lax.broadcasted_iota(jnp.int32, shape, dim)


def dot(a, b):
    return jnp.dot(a, b, preferred_element_type=F32)


def dot_nt(a, b):
    return lax.dot_general(a, b, NT, preferred_element_type=F32)


def halves(x):
    high = x.astype(BF)
    return high, (x - high.astype(F32)).astype(BF)


SLOTS = ((0, 2), (0, 1), (1, 2), (1, 1), (0, 0), (0, 2), (1, 0), (1, 2))


def in_hbm(*arrays):
    return [pltpu.with_memory_space_constraint(x, pltpu.HBM) for x in arrays]


def in_vmem(*arrays):
    return [pltpu.with_memory_space_constraint(x, pltpu.VMEM) for x in arrays]


def fetch(sem, pairs):
    copies = [pltpu.make_async_copy(src, dst, sem.at[n]) for n, (src, dst) in enumerate(pairs)]
    for copy in copies:
        copy.start()
    return copies


STEP = 8


def encode_kernel(tile_ref, x_hbm, gain_hbm, wt_hbm, mwt_hbm, out_ref, x_ref, gain_ref, wt_ref, mwt_ref, act, big, parts, sem):
    frames, height, columns, channels = x_ref.shape
    pairs = height // 2
    rows = frames * columns
    z, o = mwt_ref.shape
    taps = wt_ref.shape[0] // o
    span = lambda ref, n: ref.at[:, pl.ds(n * 2 * STEP, 2 * STEP)]
    blocks = pairs // STEP
    copies = fetch(
        sem,
        [(mwt_hbm, mwt_ref), (wt_hbm, wt_ref), (gain_hbm, gain_ref)]
        + [(span(x_hbm, n), span(x_ref, n)) for n in range(blocks)],
    )
    copies[0].wait()
    copies[1].wait()
    pick = (iota((o, taps * o), 1) % o == iota((o, taps * o), 0)).astype(BF)
    own = iota((taps * z, taps * o), 0) // z == iota((taps * z, taps * o), 1) // o
    folded = None
    for part in halves(mwt_ref[...]):
        spread = dot(part, pick)
        block = jnp.where(own, jnp.concatenate([spread] * taps, 0), 0.0).astype(BF)
        term = dot(block, wt_ref[...])
        folded = term if folded is None else folded + term
    folded = folded.astype(BF)
    nothing = jnp.zeros((z, channels), BF)
    for t in range(3):
        for slot, (a, e) in enumerate(SLOTS):
            at = (t * 8 + slot) * z
            for k in range(4):
                b = k - a
                tap = ((t * 3 + b) * 3 + e) * z
                value = folded[tap : tap + z] if 0 <= b < 3 else nothing
                big[at : at + z, k * channels : (k + 1) * channels] = value

    zero = jnp.zeros((rows, channels), BF)
    act[0, :, :channels] = zero
    act[pairs, :, channels:] = zero
    step = STEP
    copies[2].wait()
    gain = gain_ref[...].reshape(1, 1, 1, channels)
    for j in range(blocks):
        copies[3 + j].wait()
        x = x_ref[:, pl.ds(j * 2 * step, 2 * step)].astype(F32)
        energy = jnp.mean(x * x, axis=-1, keepdims=True)
        v = x * lax.rsqrt(energy + 1e-6) * gain
        v = v * (0.5 + 0.5 * jnp.tanh(0.5 * v))
        v = jnp.concatenate([v[f] for f in range(frames)], axis=1).astype(BF)
        v = v.reshape(step, 2, rows, channels)
        act[pl.ds(j * step, step), :, channels:] = v[:, 0]
        act[pl.ds(j * step + 1, step), :, :channels] = v[:, 1]

    first = tile_ref[0] == 0
    lanes = 8 * z
    chunk = 16
    for c in range(pairs // chunk):
        low = act[c * chunk : (c + 1) * chunk].reshape(chunk * rows, 2 * channels)
        high = act[c * chunk + 1 : (c + 1) * chunk + 1].reshape(chunk * rows, 2 * channels)
        out = dot_nt(low, big[:, : 2 * channels]) + dot_nt(high, big[:, 2 * channels :])
        out = out.reshape(chunk // 2, 2, frames, columns, 3 * lanes)
        part = lambda p, f, t: out[:, p, f, :, t * lanes : (t + 1) * lanes]
        for p in range(2):
            ext = (
                part(p, 0, 2),
                part(p, 0, 1) + part(p, 1, 2),
                part(p, 0, 0) + part(p, 1, 1),
                part(p, 1, 0),
            )
            slots = (
                jnp.where(first, ext[0], 0.0),
                jnp.where(first, ext[1], 0.0),
                jnp.where(first, ext[2], ext[0]),
                jnp.where(first, ext[3], ext[1]),
            )
            for f in range(4):
                at = ((p * 4 + f) * (pairs // 2) + c * chunk // 2) * columns
                size = chunk // 2 * columns
                parts[at : at + size] = slots[f].reshape(size, lanes)

    total = parts.shape[0]
    even = parts[pl.ds(0, total // 2, stride=2)]
    odd = parts[pl.ds(1, total // 2, stride=2)]
    slot = iota((1, lanes), 1) // z
    near = pltpu.roll(even, lanes - z, 1)
    far = pltpu.roll(even, lanes - 3 * z, 1)
    moved = jnp.where((slot == 0) | (slot == 2), near, jnp.where((slot == 1) | (slot == 3), far, 0.0))
    back = (slot == 5) | (slot == 7)
    out_ref[...] = jnp.where(back, even, moved + odd).astype(BF)


def prep_kernel(
    ctx_hbm, patch_hbm, pb_hbm, cb_hbm, shift_hbm, scale_hbm, noisy_hbm, mask_hbm, conv_bias_hbm, mwt_hbm, mb_hbm,
    w_ref, vec_ref, gram_ref, aux_ref, base_ref,
    ctx_ref, rows_ref, noisy_ref, conv_bias_ref, mwt_ref, mb_ref, sem,
):
    z = mwt_ref.shape[0]
    lat = 4 * z
    width = w_ref.shape[1]
    size = w_ref.shape[0]
    copies = fetch(
        sem,
        [
            (ctx_hbm.at[pl.ds(0, lat)], ctx_ref),
            (patch_hbm, w_ref.at[pl.ds(lat, lat)]),
            (ctx_hbm.at[pl.ds(lat, 2 * lat)], w_ref.at[pl.ds(2 * lat, 2 * lat)]),
            (pb_hbm, rows_ref.at[0]),
            (cb_hbm, rows_ref.at[1]),
            (shift_hbm, rows_ref.at[2]),
            (scale_hbm, rows_ref.at[3]),
            (noisy_hbm, noisy_ref),
            (mask_hbm, base_ref.at[:, pl.ds(2 * lat, 2 * lat)]),
            (conv_bias_hbm, conv_bias_ref),
            (mwt_hbm, mwt_ref),
            (mb_hbm, mb_ref),
        ],
    )
    for copy in copies:
        copy.wait()
    row, col = iota((lat, lat), 0), iota((lat, lat), 1)
    order = (col == (row % z) * 4 + row // z).astype(BF)
    w_ref[:lat] = dot(order, ctx_ref[...]).astype(BF)
    bias = rows_ref[0] + rows_ref[1]
    mean_b = jnp.mean(bias, axis=1, keepdims=True)
    centred = bias - mean_b
    vec_ref[0:1] = bias
    vec_ref[1:2] = 1.0 + rows_ref[3]
    vec_ref[2:3] = rows_ref[2]
    vec_ref[3:8] = jnp.zeros((5, width), F32)
    w = w_ref[...]
    high, low = halves(centred)
    rows = jnp.concatenate([jnp.ones((1, width), BF), high, low, jnp.zeros((5, width), BF)], 0)
    sums = dot_nt(rows, w)
    mean_w = sums[0:1] / width
    ones = jnp.ones((128, width), BF)
    mean_col = dot_nt(w, ones)[:, :1] / width
    gram = dot_nt(w, w) / width - mean_col * mean_w
    high, low = halves(gram)
    gram_ref[:, :size] = high
    gram_ref[:, size:] = low
    square = jnp.mean(centred * centred, axis=1, keepdims=True)
    tiled = jnp.concatenate([mwt_ref[...]] * 8, 0)
    conv_bias = jnp.broadcast_to(conv_bias_ref[...], (8, conv_bias_ref.shape[1]))
    latent_bias = lax.dot_general(conv_bias, tiled, NT, precision=lax.Precision.HIGHEST, preferred_element_type=F32)
    latent_bias = latent_bias[:1] + jnp.concatenate([mb_ref[...]] * 8, 1)
    aux_ref[0:1] = mean_w
    aux_ref[1:2] = 2.0 * (sums[1:2] + sums[2:3]) / width
    aux_ref[2:3] = jnp.broadcast_to(mean_b, (1, size))
    aux_ref[3:4] = jnp.broadcast_to(square, (1, size))
    aux_ref[4:5] = jnp.concatenate([latent_bias] * (size // latent_bias.shape[1]), 1)
    aux_ref[5:8] = jnp.zeros((3, size), F32)
    place = (iota((lat, 2 * lat), 1) == iota((lat, 2 * lat), 0) + lat).astype(BF)
    noisy = lax.dot_general(noisy_ref[...], place, (((0,), (0,)), ((), ())), preferred_element_type=F32)
    base_ref[:, : 2 * lat] = noisy.astype(BF)


BLOCKS = 10


def embed_kernel(arrived_ref, base_ref, w_ref, vec_ref, gram_ref, aux_ref, out_hbm, out_ref, sem):
    block = w_ref.shape[1] // BLOCKS
    columns = lambda n: pl.ds(n * block, block)
    tokens = base_ref.shape[0]
    lanes = arrived_ref.shape[1]
    z = lanes // 8
    both = arrived_ref[:tokens].astype(F32) + arrived_ref[tokens:].astype(F32)
    crossed = pltpu.roll(both, lanes // 2, 1)
    row = iota((tokens, 1), 0)
    down = jnp.where(row == 0, 0.0, pltpu.roll(crossed, 1, 0))
    up = jnp.where(row == tokens - 1, 0.0, pltpu.roll(crossed, tokens - 1, 0))
    lane = iota((1, lanes), 1)
    latent = both + jnp.where(lane // z % 2 == 0, down, up) + aux_ref[4:5, :lanes]
    front = jnp.where(lane < lanes // 2, latent, base_ref[:, :lanes].astype(F32))
    x = jnp.concatenate([front.astype(BF), base_ref[:, lanes:]], 1)
    size = x.shape[1]
    y = dot(x, gram_ref[:, :size]) + dot(x, gram_ref[:, size:])
    xf = x.astype(F32)
    mean = jnp.sum(xf * aux_ref[0:1], axis=1, keepdims=True) + aux_ref[2:3, :1]
    variance = jnp.sum((y + aux_ref[1:2]) * xf, axis=1, keepdims=True) + aux_ref[3:4, :1]
    scale = lax.rsqrt(jnp.maximum(variance, 0.0) + 1e-6)
    offset = mean * scale
    sent = []
    for n in range(BLOCKS):
        at = slice(n * block, (n + 1) * block)
        combined = dot(x, w_ref[:, at]) + vec_ref[0:1, at]
        out_ref[:, at] = ((combined * scale - offset) * vec_ref[1:2, at] + vec_ref[2:3, at]).astype(BF)
        copy = pltpu.make_async_copy(out_ref.at[:, columns(n)], out_hbm.at[:, columns(n)], sem.at[n])
        copy.start()
        sent.append(copy)
    for copy in sent:
        copy.wait()


def body(
    section_input, norm_gain, conv_weight, conv_bias, mean_weight, mean_bias, noisy_tokens, mask_tokens,
    patch_weight, patch_bias, context_weight, context_bias, norm_shift, norm_scale,
):
    frames, height, columns, channels = section_input.shape
    z = mean_weight.shape[1]
    tokens = noisy_tokens.shape[0]
    width = patch_weight.shape[1]
    features = patch_weight.shape[0] + context_weight.shape[0]
    shards = lax.axis_size("tile") * lax.axis_size("seq")
    tile = lax.axis_index("tile").astype(jnp.int32).reshape(1)
    vmem = pl.BlockSpec(memory_space=pltpu.VMEM)
    hbm = pl.BlockSpec(memory_space=pltpu.HBM)
    params = lambda mib: pltpu.CompilerParams(vmem_limit_bytes=mib * 1024 * 1024)
    row = lambda v: v.reshape(1, -1)
    taps_out = conv_weight.shape[1]
    dma = pltpu.SemaphoreType.DMA
    message = pl.pallas_call(
        encode_kernel,
        out_shape=jax.ShapeDtypeStruct((shards * 4, 8 * z), BF),
        in_specs=[pl.BlockSpec(memory_space=pltpu.SMEM)] + [hbm] * 4,
        out_specs=vmem,
        scratch_shapes=[
            pltpu.VMEM(section_input.shape, BF),
            pltpu.VMEM(norm_gain.shape, F32),
            pltpu.VMEM((taps_out, channels), BF),
            pltpu.VMEM(mean_weight.shape[::-1], F32),
            pltpu.VMEM((height // 2 + 1, frames * columns, 2 * channels), BF),
            pltpu.VMEM((3 * 8 * z, 4 * channels), BF),
            pltpu.VMEM((shards * 8, 8 * z), F32),
            dma((3 + height // 2 // STEP,)),
        ],
        compiler_params=params(24),
        name="encode",
    )(tile, *in_hbm(section_input, norm_gain, conv_weight.T, mean_weight.T))
    arrived = lax.all_to_all(message.reshape(shards, 4, 8 * z), ("tile", "seq"), 0, 0)
    arrived = arrived.reshape(shards * 4, 8 * z)
    weights, vectors, gram, aux, base = pl.pallas_call(
        prep_kernel,
        out_shape=(
            jax.ShapeDtypeStruct((features, width), BF),
            jax.ShapeDtypeStruct((8, width), F32),
            jax.ShapeDtypeStruct((features, 2 * features), BF),
            jax.ShapeDtypeStruct((8, features), F32),
            jax.ShapeDtypeStruct((tokens, features), BF),
        ),
        in_specs=[hbm] * 11,
        out_specs=(vmem,) * 5,
        scratch_shapes=[
            pltpu.VMEM((4 * z, width), BF),
            pltpu.VMEM((4, 1, width), F32),
            pltpu.VMEM(noisy_tokens.shape[::-1], BF),
            pltpu.VMEM((1, conv_bias.shape[0]), F32),
            pltpu.VMEM(mean_weight.shape[::-1], F32),
            pltpu.VMEM((1, z), F32),
            dma((12,)),
        ],
        compiler_params=params(24),
        cost_estimate=pl.CostEstimate(flops=2 * features * features * width, bytes_accessed=6_000_000, transcendentals=0),
        name="prep",
    )(
        *in_hbm(
            context_weight, patch_weight, row(patch_bias), row(context_bias), row(norm_shift), row(norm_scale),
            noisy_tokens.T, mask_tokens, row(conv_bias), mean_weight.T, row(mean_bias),
        )
    )
    return pl.pallas_call(
        embed_kernel,
        out_shape=jax.ShapeDtypeStruct((tokens, width), BF),
        in_specs=[vmem] * 6,
        out_specs=hbm,
        scratch_shapes=[
            pltpu.VMEM((tokens, width), BF),
            dma((BLOCKS,)),
        ],
        compiler_params=params(24),
        name="embed",
    )(*in_vmem(arrived, base, weights, vectors, gram, aux))


def solution(mesh):
    placed = (
        P("tile", None, "seq", None),
        P(),
        P(),
        P(),
        P(),
        P(),
        P(("seq", "tile"), None),
        P(("seq", "tile"), None),
        P(),
        P(),
        P(),
        P(),
        P(),
        P(),
    )
    return jax.shard_map(
        body, mesh=mesh, in_specs=placed, out_specs=P(("seq", "tile"), None), check_vma=False
    )
```

```python
import jax
import jax.numpy as jnp
from jax import lax
from jax.experimental import pallas as pl
from jax.experimental.pallas import tpu as pltpu
from jax.sharding import PartitionSpec as P

BF = jnp.bfloat16
F32 = jnp.float32
NT = (((1,), (1,)), ((), ()))


def iota(shape, dim):
    return lax.broadcasted_iota(jnp.int32, shape, dim)


def dot(a, b):
    return jnp.dot(a, b, preferred_element_type=F32)


def dot_nt(a, b):
    return lax.dot_general(a, b, NT, preferred_element_type=F32)


def halves(x):
    high = x.astype(BF)
    return high, (x - high.astype(F32)).astype(BF)


SLOTS = ((0, 2), (0, 1), (1, 2), (1, 1), (0, 0), (0, 2), (1, 0), (1, 2))


def in_hbm(*arrays):
    return [pltpu.with_memory_space_constraint(x, pltpu.HBM) for x in arrays]


def in_vmem(*arrays):
    return [pltpu.with_memory_space_constraint(x, pltpu.VMEM) for x in arrays]


def fetch(sem, pairs):
    copies = [pltpu.make_async_copy(src, dst, sem.at[n]) for n, (src, dst) in enumerate(pairs)]
    for copy in copies:
        copy.start()
    return copies


STEP = 8
CHUNK = 16


def encode_kernel(tile_ref, x_hbm, gain_hbm, wt_hbm, mwt_hbm, out_ref, x_ref, gain_ref, wt_ref, mwt_ref, act, big, parts, sem):
    frames, height, columns, channels = x_ref.shape
    pairs = height // 2
    rows = frames * columns
    z, o = mwt_ref.shape
    taps = wt_ref.shape[0] // o
    span = lambda ref, n: ref.at[:, pl.ds(n * 2 * STEP, 2 * STEP)]
    blocks = pairs // STEP
    copies = fetch(
        sem,
        [(mwt_hbm, mwt_ref), (wt_hbm, wt_ref), (gain_hbm, gain_ref)]
        + [(span(x_hbm, n), span(x_ref, n)) for n in range(blocks)],
    )
    for copy in copies[: 3 + blocks // 2]:
        copy.wait()
    group = 4
    pick = (iota((o, group * o), 1) % o == iota((o, group * o), 0)).astype(BF)
    own = iota((group * z, group * o), 0) // z == iota((group * z, group * o), 1) // o
    spread = [jnp.where(own, jnp.concatenate([dot(part, pick)] * group, 0), 0.0) for part in halves(mwt_ref[...])]
    spread = jnp.concatenate(spread, 0).astype(BF)
    folded = []
    for tap in range(0, taps, group):
        count = min(group, taps - tap)
        term = dot(spread[:, : count * o], wt_ref[tap * o : (tap + count) * o])
        folded.append((term[: count * z] + term[group * z : (group + count) * z]).astype(BF))
    folded = jnp.concatenate(folded, 0)
    nothing = jnp.zeros((z, channels), BF)
    for t in range(3):
        for slot, (a, e) in enumerate(SLOTS):
            at = (t * 8 + slot) * z
            for k in range(4):
                b = k - a
                tap = ((t * 3 + b) * 3 + e) * z
                value = folded[tap : tap + z] if 0 <= b < 3 else nothing
                big[at : at + z, k * channels : (k + 1) * channels] = value

    zero = jnp.zeros((rows, channels), BF)
    act[0, :, :channels] = zero
    act[pairs, :, channels:] = zero
    gain = gain_ref[...].reshape(1, 1, 1, channels)
    first = tile_ref[0] == 0
    lanes = 8 * z

    def activate(j):
        x = x_ref[:, pl.ds(j * 2 * STEP, 2 * STEP)].astype(F32)
        energy = jnp.mean(x * x, axis=-1, keepdims=True)
        v = x * lax.rsqrt(energy + 1e-6) * gain
        v = v * (0.5 + 0.5 * jnp.tanh(0.5 * v))
        v = jnp.concatenate([v[f] for f in range(frames)], axis=1).astype(BF)
        v = v.reshape(STEP, 2, rows, channels)
        act[pl.ds(j * STEP, STEP), :, channels:] = v[:, 0]
        act[pl.ds(j * STEP + 1, STEP), :, :channels] = v[:, 1]

    def convolve(c):
        low = act[c * CHUNK : (c + 1) * CHUNK].reshape(CHUNK * rows, 2 * channels)
        high = act[c * CHUNK + 1 : (c + 1) * CHUNK + 1].reshape(CHUNK * rows, 2 * channels)
        out = dot_nt(low, big[:, : 2 * channels]) + dot_nt(high, big[:, 2 * channels :])
        out = out.reshape(CHUNK // 2, 2, frames, columns, 3 * lanes)
        part = lambda p, f, t: out[:, p, f, :, t * lanes : (t + 1) * lanes]
        for p in range(2):
            ext = (
                part(p, 0, 2),
                part(p, 0, 1) + part(p, 1, 2),
                part(p, 0, 0) + part(p, 1, 1),
                part(p, 1, 0),
            )
            slots = (
                jnp.where(first, ext[0], 0.0),
                jnp.where(first, ext[1], 0.0),
                jnp.where(first, ext[2], ext[0]),
                jnp.where(first, ext[3], ext[1]),
            )
            for f in range(4):
                at = ((p * 4 + f) * (pairs // 2) + c * CHUNK // 2) * columns
                size = CHUNK // 2 * columns
                parts[at : at + size] = slots[f].reshape(size, lanes)

    done = 0
    for j in range(blocks):
        if j == blocks // 2:
            for copy in copies[3 + blocks // 2 :]:
                copy.wait()
        activate(j)
        while (done + 1) * CHUNK + 1 <= (j + 1) * STEP:
            convolve(done)
            done += 1
    while done * CHUNK < pairs:
        convolve(done)
        done += 1

    total = parts.shape[0]
    even = parts[pl.ds(0, total // 2, stride=2)]
    odd = parts[pl.ds(1, total // 2, stride=2)]
    slot = iota((1, lanes), 1) // z
    near = pltpu.roll(even, lanes - z, 1)
    far = pltpu.roll(even, lanes - 3 * z, 1)
    moved = jnp.where((slot == 0) | (slot == 2), near, jnp.where((slot == 1) | (slot == 3), far, 0.0))
    back = (slot == 5) | (slot == 7)
    out_ref[...] = jnp.where(back, even, moved + odd).astype(BF)


def prep_kernel(
    ctx_hbm, patch_hbm, pb_hbm, cb_hbm, shift_hbm, scale_hbm, noisy_hbm, mask_hbm, conv_bias_hbm, mwt_hbm, mb_hbm,
    w_ref, gram_ref, aux_ref, base_ref,
    ctx_ref, rows_ref, noisy_ref, conv_bias_ref, mwt_ref, mb_ref, sem,
):
    z = mwt_ref.shape[0]
    lat = 4 * z
    width = w_ref.shape[1]
    size = 4 * lat
    copies = fetch(
        sem,
        [
            (ctx_hbm.at[pl.ds(0, lat)], ctx_ref),
            (patch_hbm, w_ref.at[pl.ds(lat, lat)]),
            (ctx_hbm.at[pl.ds(lat, 2 * lat)], w_ref.at[pl.ds(2 * lat, 2 * lat)]),
            (pb_hbm, rows_ref.at[0]),
            (cb_hbm, rows_ref.at[1]),
            (shift_hbm, rows_ref.at[2]),
            (scale_hbm, rows_ref.at[3]),
            (noisy_hbm, noisy_ref),
            (mask_hbm, base_ref.at[:, pl.ds(2 * lat, 2 * lat)]),
            (conv_bias_hbm, conv_bias_ref),
            (mwt_hbm, mwt_ref),
            (mb_hbm, mb_ref),
        ],
    )
    for copy in copies:
        copy.wait()
    row, col = iota((lat, lat), 0), iota((lat, lat), 1)
    order = (col == (row % z) * 4 + row // z).astype(BF)
    w_ref[:lat] = dot(order, ctx_ref[...]).astype(BF)
    bias = rows_ref[0] + rows_ref[1]
    mean_b = jnp.mean(bias, axis=1, keepdims=True)
    centred = bias - mean_b
    gain = 1.0 + rows_ref[3]
    vectors = (*halves(centred * gain), *halves(rows_ref[2]))
    w_ref[size:] = jnp.concatenate([*vectors, jnp.zeros((VECTORS - 4, width), BF)], 0)
    w = w_ref[:size]
    high, low = halves(centred)
    rows = jnp.concatenate([jnp.ones((1, width), BF), high, low, jnp.zeros((5, width), BF)], 0)
    sums = dot_nt(rows, w)
    mean_w = sums[0:1] / width
    ones = jnp.ones((128, width), BF)
    mean_col = dot_nt(w, ones)[:, :1] / width
    gram = dot_nt(w, w) / width - mean_col * mean_w
    high, low = halves(gram)
    gram_ref[:, :size] = high
    gram_ref[:, size:] = low
    square = jnp.mean(centred * centred, axis=1, keepdims=True)
    tiled = jnp.concatenate([mwt_ref[...]] * 8, 0)
    conv_bias = jnp.broadcast_to(conv_bias_ref[...], (8, conv_bias_ref.shape[1]))
    latent_bias = lax.dot_general(conv_bias, tiled, NT, precision=lax.Precision.HIGHEST, preferred_element_type=F32)
    latent_bias = latent_bias[:1] + jnp.concatenate([mb_ref[...]] * 8, 1)
    aux_ref[0:1] = 2.0 * (sums[1:2] + sums[2:3]) / width
    aux_ref[1:2] = jnp.broadcast_to(square, (1, size))
    aux_ref[2:3] = jnp.concatenate([latent_bias] * (size // latent_bias.shape[1]), 1)
    aux_ref[3:8] = jnp.zeros((5, size), F32)
    w_ref[:size] = ((w.astype(F32) - mean_col) * gain).astype(BF)
    place = (iota((lat, 2 * lat), 1) == iota((lat, 2 * lat), 0) + lat).astype(BF)
    noisy = lax.dot_general(noisy_ref[...], place, (((0,), (0,)), ((), ())), preferred_element_type=F32)
    base_ref[:, : 2 * lat] = noisy.astype(BF)


VECTORS = 16
BLOCKS = 10


def embed_kernel(arrived_ref, base_ref, w_ref, gram_ref, aux_ref, out_hbm, out_ref, sem):
    block = w_ref.shape[1] // BLOCKS
    columns = lambda n: pl.ds(n * block, block)
    tokens = base_ref.shape[0]
    lanes = arrived_ref.shape[1]
    z = lanes // 8
    both = arrived_ref[:tokens].astype(F32) + arrived_ref[tokens:].astype(F32)
    crossed = pltpu.roll(both, lanes // 2, 1)
    row = iota((tokens, 1), 0)
    down = jnp.where(row == 0, 0.0, pltpu.roll(crossed, 1, 0))
    up = jnp.where(row == tokens - 1, 0.0, pltpu.roll(crossed, tokens - 1, 0))
    lane = iota((1, lanes), 1)
    latent = both + jnp.where(lane // z % 2 == 0, down, up) + aux_ref[2:3, :lanes]
    front = jnp.where(lane < lanes // 2, latent, base_ref[:, :lanes].astype(F32))
    x = jnp.concatenate([front.astype(BF), base_ref[:, lanes:]], 1)
    size = x.shape[1]
    scales = []
    for r in range(0, tokens, 256):
        xr = x[r : r + 256]
        y = dot(xr, gram_ref[:, :size]) + dot(xr, gram_ref[:, size:])
        variance = jnp.sum((y + aux_ref[0:1]) * xr.astype(F32), axis=1, keepdims=True) + aux_ref[1:2, :1]
        scales.append(lax.rsqrt(jnp.maximum(variance, 0.0) + 1e-6))
    scale = jnp.concatenate(scales, 0)
    sent = []
    for n in range(BLOCKS):
        at = slice(n * block, (n + 1) * block)
        vectors = w_ref[size:, at].astype(F32)
        centred = dot(x, w_ref[:size, at]) + (vectors[0:1] + vectors[1:2])
        out_ref[:, at] = (centred * scale + (vectors[2:3] + vectors[3:4])).astype(BF)
        copy = pltpu.make_async_copy(out_ref.at[:, columns(n)], out_hbm.at[:, columns(n)], sem.at[n])
        copy.start()
        sent.append(copy)
    for copy in sent:
        copy.wait()


def body(
    section_input, norm_gain, conv_weight, conv_bias, mean_weight, mean_bias, noisy_tokens, mask_tokens,
    patch_weight, patch_bias, context_weight, context_bias, norm_shift, norm_scale,
):
    frames, height, columns, channels = section_input.shape
    z = mean_weight.shape[1]
    tokens = noisy_tokens.shape[0]
    width = patch_weight.shape[1]
    features = patch_weight.shape[0] + context_weight.shape[0]
    shards = lax.axis_size("tile") * lax.axis_size("seq")
    tile = lax.axis_index("tile").astype(jnp.int32).reshape(1)
    vmem = pl.BlockSpec(memory_space=pltpu.VMEM)
    hbm = pl.BlockSpec(memory_space=pltpu.HBM)
    params = lambda mib: pltpu.CompilerParams(vmem_limit_bytes=mib * 1024 * 1024)
    row = lambda v: v.reshape(1, -1)
    taps_out = conv_weight.shape[1]
    dma = pltpu.SemaphoreType.DMA
    message = pl.pallas_call(
        encode_kernel,
        out_shape=jax.ShapeDtypeStruct((shards * 4, 8 * z), BF),
        in_specs=[pl.BlockSpec(memory_space=pltpu.SMEM)] + [hbm] * 4,
        out_specs=vmem,
        scratch_shapes=[
            pltpu.VMEM(section_input.shape, BF),
            pltpu.VMEM(norm_gain.shape, F32),
            pltpu.VMEM((taps_out, channels), BF),
            pltpu.VMEM(mean_weight.shape[::-1], F32),
            pltpu.VMEM((height // 2 + 1, frames * columns, 2 * channels), BF),
            pltpu.VMEM((3 * 8 * z, 4 * channels), BF),
            pltpu.VMEM((shards * 8, 8 * z), F32),
            dma((3 + height // 2 // STEP,)),
        ],
        compiler_params=params(24),
        name="encode",
    )(tile, *in_hbm(section_input, norm_gain, conv_weight.T, mean_weight.T))
    arrived = lax.all_to_all(message.reshape(shards, 4, 8 * z), ("tile", "seq"), 0, 0)
    arrived = arrived.reshape(shards * 4, 8 * z)
    weights, gram, aux, base = pl.pallas_call(
        prep_kernel,
        out_shape=(
            jax.ShapeDtypeStruct((features + VECTORS, width), BF),
            jax.ShapeDtypeStruct((features, 2 * features), BF),
            jax.ShapeDtypeStruct((8, features), F32),
            jax.ShapeDtypeStruct((tokens, features), BF),
        ),
        in_specs=[hbm] * 11,
        out_specs=(vmem,) * 4,
        scratch_shapes=[
            pltpu.VMEM((4 * z, width), BF),
            pltpu.VMEM((4, 1, width), F32),
            pltpu.VMEM(noisy_tokens.shape[::-1], BF),
            pltpu.VMEM((1, conv_bias.shape[0]), F32),
            pltpu.VMEM(mean_weight.shape[::-1], F32),
            pltpu.VMEM((1, z), F32),
            dma((12,)),
        ],
        compiler_params=params(24),
        cost_estimate=pl.CostEstimate(flops=2 * features * features * width, bytes_accessed=6_000_000, transcendentals=0),
        name="prep",
    )(
        *in_hbm(
            context_weight, patch_weight, row(patch_bias), row(context_bias), row(norm_shift), row(norm_scale),
            noisy_tokens.T, mask_tokens, row(conv_bias), mean_weight.T, row(mean_bias),
        )
    )
    return pl.pallas_call(
        embed_kernel,
        out_shape=jax.ShapeDtypeStruct((tokens, width), BF),
        in_specs=[vmem] * 5,
        out_specs=hbm,
        scratch_shapes=[
            pltpu.VMEM((tokens, width), BF),
            dma((BLOCKS,)),
        ],
        compiler_params=params(24),
        name="embed",
    )(*in_vmem(arrived, base, weights, gram, aux))


def solution(mesh):
    placed = (
        P("tile", None, "seq", None),
        P(),
        P(),
        P(),
        P(),
        P(),
        P(("seq", "tile"), None),
        P(("seq", "tile"), None),
        P(),
        P(),
        P(),
        P(),
        P(),
        P(),
    )
    return jax.shard_map(
        body, mesh=mesh, in_specs=placed, out_specs=P(("seq", "tile"), None), check_vma=False
    )
```

```python
import jax
import jax.numpy as jnp
from jax import lax
from jax.experimental import pallas as pl
from jax.experimental.pallas import tpu as pltpu
from jax.sharding import PartitionSpec as P

BF = jnp.bfloat16
F32 = jnp.float32
NT = (((1,), (1,)), ((), ()))


def iota(shape, dim):
    return lax.broadcasted_iota(jnp.int32, shape, dim)


def dot(a, b):
    return jnp.dot(a, b, preferred_element_type=F32)


def dot_nt(a, b):
    return lax.dot_general(a, b, NT, preferred_element_type=F32)


def halves(x):
    high = x.astype(BF)
    return high, (x - high.astype(F32)).astype(BF)


SLOTS = ((0, 2), (0, 1), (1, 2), (1, 1), (0, 0), (0, 2), (1, 0), (1, 2))


def in_hbm(*arrays):
    return [pltpu.with_memory_space_constraint(x, pltpu.HBM) for x in arrays]


def in_vmem(*arrays):
    return [pltpu.with_memory_space_constraint(x, pltpu.VMEM) for x in arrays]


def fetch(sem, pairs):
    copies = [pltpu.make_async_copy(src, dst, sem.at[n]) for n, (src, dst) in enumerate(pairs)]
    for copy in copies:
        copy.start()
    return copies


STEP = 8
CHUNK = 32


def encode_kernel(tile_ref, x_hbm, gain_hbm, wt_hbm, mwt_hbm, out_ref, x_ref, gain_ref, wt_ref, mwt_ref, act, big, side, parts, sem):
    frames, height, columns, channels = x_ref.shape
    pairs = height // 2
    rows = frames * columns
    z, o = mwt_ref.shape
    taps = wt_ref.shape[0] // o
    span = lambda ref, n: ref.at[:, pl.ds(n * 2 * STEP, 2 * STEP)]
    blocks = pairs // STEP
    copies = fetch(
        sem,
        [(mwt_hbm, mwt_ref), (wt_hbm, wt_ref), (gain_hbm, gain_ref)]
        + [(span(x_hbm, n), span(x_ref, n)) for n in range(blocks)],
    )
    for copy in copies[: 3 + blocks // 2]:
        copy.wait()
    group = 4
    pick = (iota((o, group * o), 1) % o == iota((o, group * o), 0)).astype(BF)
    own = iota((group * z, group * o), 0) // z == iota((group * z, group * o), 1) // o
    spread = [jnp.where(own, jnp.concatenate([dot(part, pick)] * group, 0), 0.0) for part in halves(mwt_ref[...])]
    spread = jnp.concatenate(spread, 0).astype(BF)
    folded = []
    for tap in range(0, taps, group):
        count = min(group, taps - tap)
        term = dot(spread[:, : count * o], wt_ref[tap * o : (tap + count) * o])
        folded.append((term[: count * z] + term[group * z : (group + count) * z]).astype(BF))
    folded = jnp.concatenate(folded, 0)
    nothing = jnp.zeros((z, channels), BF)
    lanes = 8 * z
    for t in range(3):
        for slot, (a, e) in enumerate(SLOTS):
            at = (t * 8 + slot) * z
            for k in range(4):
                b = k - a
                tap = ((t * 3 + b) * 3 + e) * z
                value = folded[tap : tap + z] if 0 <= b < 3 else nothing
                if t:
                    big[at - lanes : at - lanes + z, k * channels : (k + 1) * channels] = value
                else:
                    row = at + k // 2 * lanes
                    side[row : row + z, k % 2 * channels : (k % 2 + 1) * channels] = value

    zero = jnp.zeros((rows, channels), BF)
    act[0, :, :channels] = zero
    act[pairs, :, channels:] = zero
    gain = gain_ref[...].reshape(1, 1, 1, channels)
    first = tile_ref[0] == 0
    def activate(j):
        x = x_ref[:, pl.ds(j * 2 * STEP, 2 * STEP)].astype(F32)
        energy = jnp.mean(x * x, axis=-1, keepdims=True)
        v = x * lax.rsqrt(energy + 1e-6) * gain
        v = v * (0.5 + 0.5 * jnp.tanh(0.5 * v))
        v = jnp.concatenate([v[f] for f in range(frames)], axis=1).astype(BF)
        v = v.reshape(STEP, 2, rows, channels)
        act[pl.ds(j * STEP, STEP), :, channels:] = v[:, 0]
        act[pl.ds(j * STEP + 1, STEP), :, :channels] = v[:, 1]

    def convolve(c):
        both = act[c * CHUNK : (c + 1) * CHUNK + 1].reshape((CHUNK + 1) * rows, 2 * channels)
        low, high = both[:-rows], both[rows:]
        later = dot_nt(low, big[:, : 2 * channels]) + dot_nt(high, big[:, 2 * channels :])
        now = dot_nt(both, side[...])
        outs = (now[:-rows, :lanes] + now[rows:, lanes:], later[:, :lanes], later[:, lanes:])
        outs = [out.reshape(CHUNK // 2, 2, frames, columns, lanes) for out in outs]
        part = lambda p, f, t: outs[t][:, p, f]
        for p in range(2):
            ext = (
                part(p, 0, 2),
                part(p, 0, 1) + part(p, 1, 2),
                part(p, 0, 0) + part(p, 1, 1),
                part(p, 1, 0),
            )
            slots = (
                jnp.where(first, ext[0], 0.0),
                jnp.where(first, ext[1], 0.0),
                jnp.where(first, ext[2], ext[0]),
                jnp.where(first, ext[3], ext[1]),
            )
            for f in range(4):
                at = ((p * 4 + f) * (pairs // 2) + c * CHUNK // 2) * columns
                size = CHUNK // 2 * columns
                parts[at : at + size] = slots[f].reshape(size, lanes)

    done = 0
    for j in range(blocks):
        if j == blocks // 2:
            for copy in copies[3 + blocks // 2 :]:
                copy.wait()
        activate(j)
        while (done + 1) * CHUNK + 1 <= (j + 1) * STEP:
            convolve(done)
            done += 1
    while done * CHUNK < pairs:
        convolve(done)
        done += 1

    total = parts.shape[0]
    even = parts[pl.ds(0, total // 2, stride=2)]
    odd = parts[pl.ds(1, total // 2, stride=2)]
    slot = iota((1, lanes), 1) // z
    near = pltpu.roll(even, lanes - z, 1)
    far = pltpu.roll(even, lanes - 3 * z, 1)
    moved = jnp.where((slot == 0) | (slot == 2), near, jnp.where((slot == 1) | (slot == 3), far, 0.0))
    back = (slot == 5) | (slot == 7)
    out_ref[...] = jnp.where(back, even, moved + odd).astype(BF)


def prep_kernel(
    ctx_hbm, patch_hbm, pb_hbm, cb_hbm, shift_hbm, scale_hbm, noisy_hbm, mask_hbm, conv_bias_hbm, mwt_hbm, mb_hbm,
    w_ref, vec_ref, gram_ref, aux_ref, base_ref,
    ctx_ref, rows_ref, noisy_ref, conv_bias_ref, mwt_ref, mb_ref, sem,
):
    z = mwt_ref.shape[0]
    lat = 4 * z
    width = w_ref.shape[1]
    size = w_ref.shape[0]
    copies = fetch(
        sem,
        [
            (ctx_hbm.at[pl.ds(0, lat)], ctx_ref),
            (patch_hbm, w_ref.at[pl.ds(lat, lat)]),
            (ctx_hbm.at[pl.ds(lat, 2 * lat)], w_ref.at[pl.ds(2 * lat, 2 * lat)]),
            (pb_hbm, rows_ref.at[0]),
            (cb_hbm, rows_ref.at[1]),
            (shift_hbm, rows_ref.at[2]),
            (scale_hbm, rows_ref.at[3]),
            (noisy_hbm, noisy_ref),
            (mask_hbm, base_ref.at[:, pl.ds(2 * lat, 2 * lat)]),
            (conv_bias_hbm, conv_bias_ref),
            (mwt_hbm, mwt_ref),
            (mb_hbm, mb_ref),
        ],
    )
    for copy in copies:
        copy.wait()
    row, col = iota((lat, lat), 0), iota((lat, lat), 1)
    order = (col == (row % z) * 4 + row // z).astype(BF)
    w_ref[:lat] = dot(order, ctx_ref[...]).astype(BF)
    bias = rows_ref[0] + rows_ref[1]
    mean_b = jnp.mean(bias, axis=1, keepdims=True)
    centred = bias - mean_b
    gain = 1.0 + rows_ref[3]
    vec_ref[0:1] = centred * gain
    vec_ref[1:2] = rows_ref[2]
    w = w_ref[...]
    high, low = halves(centred)
    rows = jnp.concatenate([jnp.ones((1, width), BF), high, low, jnp.zeros((5, width), BF)], 0)
    sums = dot_nt(rows, w)
    mean_w = sums[0:1] / width
    ones = jnp.ones((128, width), BF)
    mean_col = dot_nt(w, ones)[:, :1] / width
    gram = dot_nt(w, w) / width - mean_col * mean_w
    high, low = halves(gram)
    gram_ref[:, :size] = high
    gram_ref[:, size:] = low
    square = jnp.mean(centred * centred, axis=1, keepdims=True)
    tiled = jnp.concatenate([mwt_ref[...]] * 8, 0)
    conv_bias = jnp.broadcast_to(conv_bias_ref[...], (8, conv_bias_ref.shape[1]))
    latent_bias = lax.dot_general(conv_bias, tiled, NT, precision=lax.Precision.HIGHEST, preferred_element_type=F32)
    latent_bias = latent_bias[:1] + jnp.concatenate([mb_ref[...]] * 8, 1)
    aux_ref[0:1] = 2.0 * (sums[1:2] + sums[2:3]) / width
    aux_ref[1:2] = jnp.broadcast_to(square, (1, size))
    aux_ref[2:3] = jnp.concatenate([latent_bias] * (size // latent_bias.shape[1]), 1)
    aux_ref[3:8] = jnp.zeros((5, size), F32)
    w_ref[...] = ((w.astype(F32) - mean_col) * gain).astype(BF)
    place = (iota((lat, 2 * lat), 1) == iota((lat, 2 * lat), 0) + lat).astype(BF)
    noisy = lax.dot_general(noisy_ref[...], place, (((0,), (0,)), ((), ())), preferred_element_type=F32)
    base_ref[:, : 2 * lat] = noisy.astype(BF)


BLOCKS = 10


def embed_kernel(arrived_ref, base_ref, w_ref, vec_ref, gram_ref, aux_ref, out_hbm, out_ref, sem):
    block = w_ref.shape[1] // BLOCKS
    columns = lambda n: pl.ds(n * block, block)
    tokens = base_ref.shape[0]
    lanes = arrived_ref.shape[1]
    z = lanes // 8
    both = arrived_ref[:tokens].astype(F32) + arrived_ref[tokens:].astype(F32)
    crossed = pltpu.roll(both, lanes // 2, 1)
    row = iota((tokens, 1), 0)
    down = jnp.where(row == 0, 0.0, pltpu.roll(crossed, 1, 0))
    up = jnp.where(row == tokens - 1, 0.0, pltpu.roll(crossed, tokens - 1, 0))
    lane = iota((1, lanes), 1)
    latent = both + jnp.where(lane // z % 2 == 0, down, up) + aux_ref[2:3, :lanes]
    front = jnp.where(lane < lanes // 2, latent, base_ref[:, :lanes].astype(F32))
    x = jnp.concatenate([front.astype(BF), base_ref[:, lanes:]], 1)
    size = x.shape[1]
    scales = []
    for r in range(0, tokens, 256):
        xr = x[r : r + 256]
        y = dot(xr, gram_ref[:, :size]) + dot(xr, gram_ref[:, size:])
        variance = jnp.sum((y + aux_ref[0:1]) * xr.astype(F32), axis=1, keepdims=True) + aux_ref[1:2, :1]
        scales.append(lax.rsqrt(jnp.maximum(variance, 0.0) + 1e-6))
    scale = jnp.concatenate(scales, 0)
    sent = []
    for n in range(BLOCKS):
        at = slice(n * block, (n + 1) * block)
        centred = dot(x, w_ref[:, at]) + vec_ref[0:1, at]
        out_ref[:, at] = (centred * scale + vec_ref[1:2, at]).astype(BF)
        copy = pltpu.make_async_copy(out_ref.at[:, columns(n)], out_hbm.at[:, columns(n)], sem.at[n])
        copy.start()
        sent.append(copy)
    for copy in sent:
        copy.wait()


def body(
    section_input, norm_gain, conv_weight, conv_bias, mean_weight, mean_bias, noisy_tokens, mask_tokens,
    patch_weight, patch_bias, context_weight, context_bias, norm_shift, norm_scale,
):
    frames, height, columns, channels = section_input.shape
    z = mean_weight.shape[1]
    tokens = noisy_tokens.shape[0]
    width = patch_weight.shape[1]
    features = patch_weight.shape[0] + context_weight.shape[0]
    shards = lax.axis_size("tile") * lax.axis_size("seq")
    tile = lax.axis_index("tile").astype(jnp.int32).reshape(1)
    vmem = pl.BlockSpec(memory_space=pltpu.VMEM)
    hbm = pl.BlockSpec(memory_space=pltpu.HBM)
    params = lambda mib: pltpu.CompilerParams(vmem_limit_bytes=mib * 1024 * 1024)
    row = lambda v: v.reshape(1, -1)
    taps_out = conv_weight.shape[1]
    dma = pltpu.SemaphoreType.DMA
    message = pl.pallas_call(
        encode_kernel,
        out_shape=jax.ShapeDtypeStruct((shards * 4, 8 * z), BF),
        in_specs=[pl.BlockSpec(memory_space=pltpu.SMEM)] + [hbm] * 4,
        out_specs=vmem,
        scratch_shapes=[
            pltpu.VMEM(section_input.shape, BF),
            pltpu.VMEM(norm_gain.shape, F32),
            pltpu.VMEM((taps_out, channels), BF),
            pltpu.VMEM(mean_weight.shape[::-1], F32),
            pltpu.VMEM((height // 2 + 1, frames * columns, 2 * channels), BF),
            pltpu.VMEM((2 * 8 * z, 4 * channels), BF),
            pltpu.VMEM((2 * 8 * z, 2 * channels), BF),
            pltpu.VMEM((shards * 8, 8 * z), F32),
            dma((3 + height // 2 // STEP,)),
        ],
        compiler_params=params(24),
        name="encode",
    )(tile, *in_hbm(section_input, norm_gain, conv_weight.T, mean_weight.T))
    arrived = lax.all_to_all(message.reshape(shards, 4, 8 * z), ("tile", "seq"), 0, 0)
    arrived = arrived.reshape(shards * 4, 8 * z)
    weights, vectors, gram, aux, base = pl.pallas_call(
        prep_kernel,
        out_shape=(
            jax.ShapeDtypeStruct((features, width), BF),
            jax.ShapeDtypeStruct((2, width), F32),
            jax.ShapeDtypeStruct((features, 2 * features), BF),
            jax.ShapeDtypeStruct((8, features), F32),
            jax.ShapeDtypeStruct((tokens, features), BF),
        ),
        in_specs=[hbm] * 11,
        out_specs=(vmem,) * 5,
        scratch_shapes=[
            pltpu.VMEM((4 * z, width), BF),
            pltpu.VMEM((4, 1, width), F32),
            pltpu.VMEM(noisy_tokens.shape[::-1], BF),
            pltpu.VMEM((1, conv_bias.shape[0]), F32),
            pltpu.VMEM(mean_weight.shape[::-1], F32),
            pltpu.VMEM((1, z), F32),
            dma((12,)),
        ],
        compiler_params=params(24),
        cost_estimate=pl.CostEstimate(flops=2 * features * features * width, bytes_accessed=6_000_000, transcendentals=0),
        name="prep",
    )(
        *in_hbm(
            context_weight, patch_weight, row(patch_bias), row(context_bias), row(norm_shift), row(norm_scale),
            noisy_tokens.T, mask_tokens, row(conv_bias), mean_weight.T, row(mean_bias),
        )
    )
    return pl.pallas_call(
        embed_kernel,
        out_shape=jax.ShapeDtypeStruct((tokens, width), BF),
        in_specs=[vmem] * 6,
        out_specs=hbm,
        scratch_shapes=[
            pltpu.VMEM((tokens, width), BF),
            dma((BLOCKS,)),
        ],
        compiler_params=params(24),
        name="embed",
    )(*in_vmem(arrived, base, weights, vectors, gram, aux))


def solution(mesh):
    placed = (
        P("tile", None, "seq", None),
        P(),
        P(),
        P(),
        P(),
        P(),
        P(("seq", "tile"), None),
        P(("seq", "tile"), None),
        P(),
        P(),
        P(),
        P(),
        P(),
        P(),
    )
    return jax.shard_map(
        body, mesh=mesh, in_specs=placed, out_specs=P(("seq", "tile"), None), check_vma=False
    )
```

```python
import jax
import jax.numpy as jnp
from jax import lax
from jax.experimental import pallas as pl
from jax.experimental.pallas import tpu as pltpu
from jax.sharding import PartitionSpec as P

BF = jnp.bfloat16
F32 = jnp.float32
NT = (((1,), (1,)), ((), ()))


def iota(shape, dim):
    return lax.broadcasted_iota(jnp.int32, shape, dim)


def dot(a, b):
    return jnp.dot(a, b, preferred_element_type=F32)


def dot_nt(a, b):
    return lax.dot_general(a, b, NT, preferred_element_type=F32)


def halves(x):
    high = x.astype(BF)
    return high, (x - high.astype(F32)).astype(BF)


SLOTS = ((0, 2), (0, 1), (1, 2), (1, 1), (0, 0), (0, 2), (1, 0), (1, 2))


def in_hbm(*arrays):
    return [pltpu.with_memory_space_constraint(x, pltpu.HBM) for x in arrays]


def in_vmem(*arrays):
    return [pltpu.with_memory_space_constraint(x, pltpu.VMEM) for x in arrays]


def fetch(sem, pairs):
    copies = [pltpu.make_async_copy(src, dst, sem.at[n]) for n, (src, dst) in enumerate(pairs)]
    for copy in copies:
        copy.start()
    return copies


STEP = 8
CHUNK = 32


def encode_kernel(tile_ref, x_hbm, gain_hbm, wt_hbm, mwt_hbm, out_ref, x_ref, gain_ref, wt_ref, mwt_ref, act, big, side, parts, sem):
    frames, height, columns, channels = x_ref.shape
    pairs = height // 2
    rows = frames * columns
    z, o = mwt_ref.shape
    taps = wt_ref.shape[0] // o
    span = lambda ref, n: ref.at[:, pl.ds(n * 2 * STEP, 2 * STEP)]
    blocks = pairs // STEP
    copies = fetch(
        sem,
        [(mwt_hbm, mwt_ref), (wt_hbm, wt_ref), (gain_hbm, gain_ref)]
        + [(span(x_hbm, n), span(x_ref, n)) for n in range(blocks)],
    )
    for copy in copies[: 3 + 2]:
        copy.wait()
    group = 4
    pick = (iota((o, group * o), 1) % o == iota((o, group * o), 0)).astype(BF)
    own = iota((group * z, group * o), 0) // z == iota((group * z, group * o), 1) // o
    spread = [jnp.where(own, jnp.concatenate([dot(part, pick)] * group, 0), 0.0) for part in halves(mwt_ref[...])]
    spread = jnp.concatenate(spread, 0).astype(BF)
    folded = []
    for tap in range(0, taps, group):
        count = min(group, taps - tap)
        term = dot(spread[:, : count * o], wt_ref[tap * o : (tap + count) * o])
        folded.append((term[: count * z] + term[group * z : (group + count) * z]).astype(BF))
    folded = jnp.concatenate(folded, 0)
    nothing = jnp.zeros((z, channels), BF)
    lanes = 8 * z
    for t in range(3):
        for slot, (a, e) in enumerate(SLOTS):
            at = (t * 8 + slot) * z
            for k in range(4):
                b = k - a
                tap = ((t * 3 + b) * 3 + e) * z
                value = folded[tap : tap + z] if 0 <= b < 3 else nothing
                if t:
                    big[at - lanes : at - lanes + z, k * channels : (k + 1) * channels] = value
                else:
                    row = at + k // 2 * lanes
                    side[row : row + z, k % 2 * channels : (k % 2 + 1) * channels] = value

    zero = jnp.zeros((rows, channels), BF)
    act[0, :, :channels] = zero
    act[pairs, :, channels:] = zero
    gain = 0.5 * gain_ref[...].reshape(1, 1, 1, channels)
    first = tile_ref[0] == 0
    def activate(j):
        x = x_ref[:, pl.ds(j * 2 * STEP, 2 * STEP)].astype(F32)
        energy = jnp.mean(x * x, axis=-1, keepdims=True)
        u = x * lax.rsqrt(energy + 1e-6) * gain
        v = u + u * jnp.tanh(u)
        v = jnp.concatenate([v[f] for f in range(frames)], axis=1).astype(BF)
        v = v.reshape(STEP, 2, rows, channels)
        act[pl.ds(j * STEP, STEP), :, channels:] = v[:, 0]
        act[pl.ds(j * STEP + 1, STEP), :, :channels] = v[:, 1]

    def convolve(c):
        both = act[c * CHUNK : (c + 1) * CHUNK + 1].reshape((CHUNK + 1) * rows, 2 * channels)
        low, high = both[:-rows], both[rows:]
        later = dot_nt(low, big[:, : 2 * channels]) + dot_nt(high, big[:, 2 * channels :])
        now = dot_nt(both, side[...])
        outs = (now[:-rows, :lanes] + now[rows:, lanes:], later[:, :lanes], later[:, lanes:])
        outs = [out.reshape(CHUNK // 2, 2, frames, columns, lanes) for out in outs]
        part = lambda p, f, t: outs[t][:, p, f]
        for p in range(2):
            ext = (
                part(p, 0, 2),
                part(p, 0, 1) + part(p, 1, 2),
                part(p, 0, 0) + part(p, 1, 1),
                part(p, 1, 0),
            )
            slots = (
                jnp.where(first, ext[0], 0.0),
                jnp.where(first, ext[1], 0.0),
                jnp.where(first, ext[2], ext[0]),
                jnp.where(first, ext[3], ext[1]),
            )
            for f in range(4):
                at = ((p * 4 + f) * (pairs // 2) + c * CHUNK // 2) * columns
                size = CHUNK // 2 * columns
                parts[at : at + size] = slots[f].reshape(size, lanes)

    done = 0
    for j in range(blocks):
        if j == 2:
            for copy in copies[3 + 2 :]:
                copy.wait()
        activate(j)
        while (done + 1) * CHUNK + 1 <= (j + 1) * STEP:
            convolve(done)
            done += 1
    while done * CHUNK < pairs:
        convolve(done)
        done += 1

    total = parts.shape[0]
    even = parts[pl.ds(0, total // 2, stride=2)]
    odd = parts[pl.ds(1, total // 2, stride=2)]
    slot = iota((1, lanes), 1) // z
    near = pltpu.roll(even, lanes - z, 1)
    far = pltpu.roll(even, lanes - 3 * z, 1)
    moved = jnp.where((slot == 0) | (slot == 2), near, jnp.where((slot == 1) | (slot == 3), far, 0.0))
    back = (slot == 5) | (slot == 7)
    out_ref[...] = jnp.where(back, even, moved + odd).astype(BF)


def prep_kernel(
    ctx_hbm, patch_hbm, pb_hbm, cb_hbm, shift_hbm, scale_hbm, noisy_hbm, mask_hbm, conv_bias_hbm, mwt_hbm, mb_hbm,
    w_ref, vec_ref, gram_ref, aux_ref, base_ref,
    ctx_ref, rows_ref, noisy_ref, conv_bias_ref, mwt_ref, mb_ref, sem,
):
    z = mwt_ref.shape[0]
    lat = 4 * z
    width = w_ref.shape[1]
    size = w_ref.shape[0]
    copies = fetch(
        sem,
        [
            (ctx_hbm.at[pl.ds(0, lat)], ctx_ref),
            (patch_hbm, w_ref.at[pl.ds(lat, lat)]),
            (ctx_hbm.at[pl.ds(lat, 2 * lat)], w_ref.at[pl.ds(2 * lat, 2 * lat)]),
            (pb_hbm, rows_ref.at[0]),
            (cb_hbm, rows_ref.at[1]),
            (shift_hbm, rows_ref.at[2]),
            (scale_hbm, rows_ref.at[3]),
            (noisy_hbm, noisy_ref),
            (mask_hbm, base_ref.at[:, pl.ds(2 * lat, 2 * lat)]),
            (conv_bias_hbm, conv_bias_ref),
            (mwt_hbm, mwt_ref),
            (mb_hbm, mb_ref),
        ],
    )
    for copy in copies:
        copy.wait()
    row, col = iota((lat, lat), 0), iota((lat, lat), 1)
    order = (col == (row % z) * 4 + row // z).astype(BF)
    w_ref[:lat] = dot(order, ctx_ref[...]).astype(BF)
    bias = rows_ref[0] + rows_ref[1]
    mean_b = jnp.mean(bias, axis=1, keepdims=True)
    centred = bias - mean_b
    gain = 1.0 + rows_ref[3]
    vec_ref[0:1] = centred * gain
    vec_ref[1:2] = rows_ref[2]
    w = w_ref[...]
    high, low = halves(centred)
    rows = jnp.concatenate([jnp.ones((1, width), BF), high, low, jnp.zeros((5, width), BF)], 0)
    sums = dot_nt(rows, w)
    mean_w = sums[0:1] / width
    ones = jnp.ones((128, width), BF)
    mean_col = dot_nt(w, ones)[:, :1] / width
    gram = dot_nt(w, w) / width - mean_col * mean_w
    high, low = halves(gram)
    gram_ref[:, :size] = high
    gram_ref[:, size:] = low
    square = jnp.mean(centred * centred, axis=1, keepdims=True)
    tiled = jnp.concatenate([mwt_ref[...]] * 8, 0)
    conv_bias = jnp.broadcast_to(conv_bias_ref[...], (8, conv_bias_ref.shape[1]))
    latent_bias = lax.dot_general(conv_bias, tiled, NT, precision=lax.Precision.HIGHEST, preferred_element_type=F32)
    latent_bias = latent_bias[:1] + jnp.concatenate([mb_ref[...]] * 8, 1)
    aux_ref[0:1] = 2.0 * (sums[1:2] + sums[2:3]) / width
    aux_ref[1:2] = jnp.broadcast_to(square, (1, size))
    aux_ref[2:3] = jnp.concatenate([latent_bias] * (size // latent_bias.shape[1]), 1)
    aux_ref[3:8] = jnp.zeros((5, size), F32)
    w_ref[...] = ((w.astype(F32) - mean_col) * gain).astype(BF)
    place = (iota((lat, 2 * lat), 1) == iota((lat, 2 * lat), 0) + lat).astype(BF)
    noisy = lax.dot_general(noisy_ref[...], place, (((0,), (0,)), ((), ())), preferred_element_type=F32)
    base_ref[:, : 2 * lat] = noisy.astype(BF)


BLOCKS = 10


def embed_kernel(arrived_ref, base_ref, w_ref, vec_ref, gram_ref, aux_ref, out_hbm, out_ref, sem):
    block = w_ref.shape[1] // BLOCKS
    columns = lambda n: pl.ds(n * block, block)
    tokens = base_ref.shape[0]
    lanes = arrived_ref.shape[1]
    z = lanes // 8
    both = arrived_ref[:tokens].astype(F32) + arrived_ref[tokens:].astype(F32)
    crossed = pltpu.roll(both, lanes // 2, 1)
    row = iota((tokens, 1), 0)
    down = jnp.where(row == 0, 0.0, pltpu.roll(crossed, 1, 0))
    up = jnp.where(row == tokens - 1, 0.0, pltpu.roll(crossed, tokens - 1, 0))
    lane = iota((1, lanes), 1)
    latent = both + jnp.where(lane // z % 2 == 0, down, up) + aux_ref[2:3, :lanes]
    front = jnp.where(lane < lanes // 2, latent, base_ref[:, :lanes].astype(F32))
    x = jnp.concatenate([front.astype(BF), base_ref[:, lanes:]], 1)
    size = x.shape[1]
    scales = []
    for r in range(0, tokens, 256):
        xr = x[r : r + 256]
        y = dot(xr, gram_ref[:, :size]) + dot(xr, gram_ref[:, size:])
        variance = jnp.sum((y + aux_ref[0:1]) * xr.astype(F32), axis=1, keepdims=True) + aux_ref[1:2, :1]
        scales.append(lax.rsqrt(jnp.maximum(variance, 0.0) + 1e-6))
    scale = jnp.concatenate(scales, 0)
    sent = []
    for n in range(BLOCKS):
        at = slice(n * block, (n + 1) * block)
        centred = dot(x, w_ref[:, at]) + vec_ref[0:1, at]
        out_ref[:, at] = (centred * scale + vec_ref[1:2, at]).astype(BF)
        copy = pltpu.make_async_copy(out_ref.at[:, columns(n)], out_hbm.at[:, columns(n)], sem.at[n])
        copy.start()
        sent.append(copy)
    for copy in sent:
        copy.wait()


def body(
    section_input, norm_gain, conv_weight, conv_bias, mean_weight, mean_bias, noisy_tokens, mask_tokens,
    patch_weight, patch_bias, context_weight, context_bias, norm_shift, norm_scale,
):
    frames, height, columns, channels = section_input.shape
    z = mean_weight.shape[1]
    tokens = noisy_tokens.shape[0]
    width = patch_weight.shape[1]
    features = patch_weight.shape[0] + context_weight.shape[0]
    shards = lax.axis_size("tile") * lax.axis_size("seq")
    tile = lax.axis_index("tile").astype(jnp.int32).reshape(1)
    vmem = pl.BlockSpec(memory_space=pltpu.VMEM)
    hbm = pl.BlockSpec(memory_space=pltpu.HBM)
    params = lambda mib: pltpu.CompilerParams(vmem_limit_bytes=mib * 1024 * 1024)
    row = lambda v: v.reshape(1, -1)
    taps_out = conv_weight.shape[1]
    dma = pltpu.SemaphoreType.DMA
    message = pl.pallas_call(
        encode_kernel,
        out_shape=jax.ShapeDtypeStruct((shards * 4, 8 * z), BF),
        in_specs=[pl.BlockSpec(memory_space=pltpu.SMEM)] + [hbm] * 4,
        out_specs=vmem,
        scratch_shapes=[
            pltpu.VMEM(section_input.shape, BF),
            pltpu.VMEM(norm_gain.shape, F32),
            pltpu.VMEM((taps_out, channels), BF),
            pltpu.VMEM(mean_weight.shape[::-1], F32),
            pltpu.VMEM((height // 2 + 1, frames * columns, 2 * channels), BF),
            pltpu.VMEM((2 * 8 * z, 4 * channels), BF),
            pltpu.VMEM((2 * 8 * z, 2 * channels), BF),
            pltpu.VMEM((shards * 8, 8 * z), F32),
            dma((3 + height // 2 // STEP,)),
        ],
        compiler_params=params(24),
        name="encode",
    )(tile, *in_hbm(section_input, norm_gain, conv_weight.T, mean_weight.T))
    arrived = lax.all_to_all(message.reshape(shards, 4, 8 * z), ("tile", "seq"), 0, 0)
    arrived = arrived.reshape(shards * 4, 8 * z)
    weights, vectors, gram, aux, base = pl.pallas_call(
        prep_kernel,
        out_shape=(
            jax.ShapeDtypeStruct((features, width), BF),
            jax.ShapeDtypeStruct((2, width), F32),
            jax.ShapeDtypeStruct((features, 2 * features), BF),
            jax.ShapeDtypeStruct((8, features), F32),
            jax.ShapeDtypeStruct((tokens, features), BF),
        ),
        in_specs=[hbm] * 11,
        out_specs=(vmem,) * 5,
        scratch_shapes=[
            pltpu.VMEM((4 * z, width), BF),
            pltpu.VMEM((4, 1, width), F32),
            pltpu.VMEM(noisy_tokens.shape[::-1], BF),
            pltpu.VMEM((1, conv_bias.shape[0]), F32),
            pltpu.VMEM(mean_weight.shape[::-1], F32),
            pltpu.VMEM((1, z), F32),
            dma((12,)),
        ],
        compiler_params=params(24),
        cost_estimate=pl.CostEstimate(flops=2 * features * features * width, bytes_accessed=6_000_000, transcendentals=0),
        name="prep",
    )(
        *in_hbm(
            context_weight, patch_weight, row(patch_bias), row(context_bias), row(norm_shift), row(norm_scale),
            noisy_tokens.T, mask_tokens, row(conv_bias), mean_weight.T, row(mean_bias),
        )
    )
    return pl.pallas_call(
        embed_kernel,
        out_shape=jax.ShapeDtypeStruct((tokens, width), BF),
        in_specs=[vmem] * 6,
        out_specs=hbm,
        scratch_shapes=[
            pltpu.VMEM((tokens, width), BF),
            dma((BLOCKS,)),
        ],
        compiler_params=params(24),
        name="embed",
    )(*in_vmem(arrived, base, weights, vectors, gram, aux))


def solution(mesh):
    placed = (
        P("tile", None, "seq", None),
        P(),
        P(),
        P(),
        P(),
        P(),
        P(("seq", "tile"), None),
        P(("seq", "tile"), None),
        P(),
        P(),
        P(),
        P(),
        P(),
        P(),
    )
    return jax.shard_map(
        body, mesh=mesh, in_specs=placed, out_specs=P(("seq", "tile"), None), check_vma=False
    )
```

```python
import jax
import jax.numpy as jnp
from jax import lax
from jax.experimental import pallas as pl
from jax.experimental.pallas import tpu as pltpu
from jax.sharding import PartitionSpec as P

BF = jnp.bfloat16
F32 = jnp.float32
NT = (((1,), (1,)), ((), ()))


def iota(shape, dim):
    return lax.broadcasted_iota(jnp.int32, shape, dim)


def dot(a, b):
    return jnp.dot(a, b, preferred_element_type=F32)


def dot_nt(a, b):
    return lax.dot_general(a, b, NT, preferred_element_type=F32)


def halves(x):
    high = x.astype(BF)
    return high, (x - high.astype(F32)).astype(BF)


SLOTS = ((0, 2), (0, 1), (1, 2), (1, 1), (0, 0), (0, 2), (1, 0), (1, 2))


def in_hbm(*arrays):
    return [pltpu.with_memory_space_constraint(x, pltpu.HBM) for x in arrays]


def in_vmem(*arrays):
    return [pltpu.with_memory_space_constraint(x, pltpu.VMEM) for x in arrays]


def fetch(sem, pairs):
    copies = [pltpu.make_async_copy(src, dst, sem.at[n]) for n, (src, dst) in enumerate(pairs)]
    for copy in copies:
        copy.start()
    return copies


STEP = 8
CHUNK = 32


def encode_kernel(tile_ref, x_hbm, gain_hbm, wt_hbm, mwt_hbm, out_ref, x_ref, gain_ref, wt_ref, mwt_ref, act, big, side, parts, sem):
    frames, height, columns, channels = x_ref.shape
    pairs = height // 2
    rows = frames * columns
    z, o = mwt_ref.shape
    taps = wt_ref.shape[0] // o
    span = lambda ref, n: ref.at[:, pl.ds(n * 2 * STEP, 2 * STEP)]
    blocks = pairs // STEP
    copies = fetch(
        sem,
        [(mwt_hbm, mwt_ref), (wt_hbm, wt_ref), (gain_hbm, gain_ref)]
        + [(span(x_hbm, n), span(x_ref, n)) for n in range(blocks)],
    )
    for copy in copies[: 3 + 2]:
        copy.wait()
    group = 4
    pick = (iota((o, group * o), 1) % o == iota((o, group * o), 0)).astype(BF)
    own = iota((group * z, group * o), 0) // z == iota((group * z, group * o), 1) // o
    spread = [jnp.where(own, jnp.concatenate([dot(part, pick)] * group, 0), 0.0) for part in halves(mwt_ref[...])]
    spread = jnp.concatenate(spread, 0).astype(BF)
    folded = []
    for tap in range(0, taps, group):
        count = min(group, taps - tap)
        term = dot(spread[:, : count * o], wt_ref[tap * o : (tap + count) * o])
        folded.append((term[: count * z] + term[group * z : (group + count) * z]).astype(BF))
    folded = jnp.concatenate(folded, 0)
    nothing = jnp.zeros((z, channels), BF)
    lanes = 8 * z
    for t in range(3):
        for slot, (a, e) in enumerate(SLOTS):
            at = (t * 8 + slot) * z
            for k in range(4):
                b = k - a
                tap = ((t * 3 + b) * 3 + e) * z
                value = folded[tap : tap + z] if 0 <= b < 3 else nothing
                if t:
                    big[at - lanes : at - lanes + z, k * channels : (k + 1) * channels] = value
                else:
                    row = at + k // 2 * lanes
                    side[row : row + z, k % 2 * channels : (k % 2 + 1) * channels] = value

    zero = jnp.zeros((rows, channels), BF)
    act[0, :, :channels] = zero
    act[pairs, :, channels:] = zero
    gain = 0.5 * gain_ref[...].reshape(1, 1, 1, channels)
    first = tile_ref[0] == 0
    def activate(j):
        x = x_ref[:, pl.ds(j * 2 * STEP, 2 * STEP)].astype(F32)
        energy = jnp.mean(x * x, axis=-1, keepdims=True)
        u = x * lax.rsqrt(energy + 1e-6) * gain
        v = u + u * jnp.tanh(u)
        v = jnp.concatenate([v[f] for f in range(frames)], axis=1).astype(BF)
        v = v.reshape(STEP, 2, rows, channels)
        act[pl.ds(j * STEP, STEP), :, channels:] = v[:, 0]
        act[pl.ds(j * STEP + 1, STEP), :, :channels] = v[:, 1]

    def convolve(c):
        both = act[c * CHUNK : (c + 1) * CHUNK + 1].reshape((CHUNK + 1) * rows, 2 * channels)
        low, high = both[:-rows], both[rows:]
        later = dot_nt(low, big[:, : 2 * channels]) + dot_nt(high, big[:, 2 * channels :])
        now = dot_nt(both, side[...])
        outs = (now[:-rows, :lanes] + now[rows:, lanes:], later[:, :lanes], later[:, lanes:])
        outs = [out.reshape(CHUNK // 2, 2, frames, columns, lanes) for out in outs]
        part = lambda p, f, t: outs[t][:, p, f]
        for p in range(2):
            ext = (
                part(p, 0, 2),
                part(p, 0, 1) + part(p, 1, 2),
                part(p, 0, 0) + part(p, 1, 1),
                part(p, 1, 0),
            )
            slots = (
                jnp.where(first, ext[0], 0.0),
                jnp.where(first, ext[1], 0.0),
                jnp.where(first, ext[2], ext[0]),
                jnp.where(first, ext[3], ext[1]),
            )
            for f in range(4):
                at = ((p * 4 + f) * (pairs // 2) + c * CHUNK // 2) * columns
                size = CHUNK // 2 * columns
                parts[at : at + size] = slots[f].reshape(size, lanes)

    done = 0
    for j in range(blocks):
        if j == 2:
            for copy in copies[3 + 2 :]:
                copy.wait()
        activate(j)
        while (done + 1) * CHUNK + 1 <= (j + 1) * STEP:
            convolve(done)
            done += 1
    while done * CHUNK < pairs:
        convolve(done)
        done += 1

    total = parts.shape[0]
    even = parts[pl.ds(0, total // 2, stride=2)]
    odd = parts[pl.ds(1, total // 2, stride=2)]
    slot = iota((1, lanes), 1) // z
    near = pltpu.roll(even, lanes - z, 1)
    far = pltpu.roll(even, lanes - 3 * z, 1)
    moved = jnp.where((slot == 0) | (slot == 2), near, jnp.where((slot == 1) | (slot == 3), far, 0.0))
    back = (slot == 5) | (slot == 7)
    out_ref[...] = jnp.where(back, even, moved + odd).astype(BF)


def prep_kernel(
    ctx_hbm, patch_hbm, pb_hbm, cb_hbm, shift_hbm, scale_hbm, noisy_hbm, mask_hbm, conv_bias_hbm, mwt_hbm, mb_hbm,
    w_ref, vec_ref, gram_ref, aux_ref, base_ref, cross_ref,
    mask_ref, ctx_ref, rows_ref, noisy_ref, conv_bias_ref, mwt_ref, mb_ref, sem,
):
    z = mwt_ref.shape[0]
    lat = 4 * z
    width = w_ref.shape[1]
    size = w_ref.shape[0]
    copies = fetch(
        sem,
        [
            (ctx_hbm.at[pl.ds(0, lat)], ctx_ref),
            (patch_hbm, w_ref.at[pl.ds(lat, lat)]),
            (ctx_hbm.at[pl.ds(lat, 2 * lat)], w_ref.at[pl.ds(2 * lat, 2 * lat)]),
            (pb_hbm, rows_ref.at[0]),
            (cb_hbm, rows_ref.at[1]),
            (shift_hbm, rows_ref.at[2]),
            (scale_hbm, rows_ref.at[3]),
            (noisy_hbm, noisy_ref),
            (mask_hbm, mask_ref),
            (conv_bias_hbm, conv_bias_ref),
            (mwt_hbm, mwt_ref),
            (mb_hbm, mb_ref),
        ],
    )
    for copy in copies:
        copy.wait()
    row, col = iota((lat, lat), 0), iota((lat, lat), 1)
    order = (col == (row % z) * 4 + row // z).astype(BF)
    w_ref[:lat] = dot(order, ctx_ref[...]).astype(BF)
    bias = rows_ref[0] + rows_ref[1]
    mean_b = jnp.mean(bias, axis=1, keepdims=True)
    centred = bias - mean_b
    gain = 1.0 + rows_ref[3]
    vec_ref[0:1] = centred * gain
    vec_ref[1:2] = rows_ref[2]
    w = w_ref[...]
    high, low = halves(centred)
    rows = jnp.concatenate([jnp.ones((1, width), BF), high, low, jnp.zeros((5, width), BF)], 0)
    sums = dot_nt(rows, w)
    mean_w = sums[0:1] / width
    ones = jnp.ones((128, width), BF)
    mean_col = dot_nt(w, ones)[:, :1] / width
    gram = dot_nt(w, w) / width - mean_col * mean_w
    high, low = halves(gram)
    half = 2 * lat
    inside = (iota((half, half), 0) < lat) & (iota((half, half), 1) < lat)
    nil = jnp.zeros((half, half), BF)
    gram_ref[:half] = jnp.where(inside, high[:half, :half], nil)
    gram_ref[half:] = jnp.where(inside, low[:half, :half], nil)
    place = (iota((lat, half), 1) == iota((lat, half), 0) + lat).astype(BF)
    noisy = lax.dot_general(noisy_ref[...], place, (((0,), (0,)), ((), ())), preferred_element_type=F32).astype(BF)
    base_ref[:, :half] = noisy
    local = jnp.concatenate([noisy, mask_ref[...]], 1)
    base_ref[:, half:] = mask_ref[...]
    linear = 2.0 * (sums[1:2] + sums[2:3]) / width
    square = jnp.mean(centred * centred, axis=1, keepdims=True)
    tokens = local.shape[0]
    for r in range(0, tokens, tokens // 2):
        part = local[r : r + tokens // 2]
        y = dot(part, high) + dot(part, low)
        alone = jnp.sum((y + linear) * part.astype(F32), axis=1, keepdims=True) + square
        lane = iota((1, half), 1)
        cross_ref[r : r + tokens // 2] = jnp.where(
            lane < lat, 2.0 * y[:, :half] + linear[:, :half], jnp.where(lane == lat, alone, 0.0)
        )
    tiled = jnp.concatenate([mwt_ref[...]] * 8, 0)
    conv_bias = jnp.broadcast_to(conv_bias_ref[...], (8, conv_bias_ref.shape[1]))
    latent_bias = lax.dot_general(conv_bias, tiled, NT, precision=lax.Precision.HIGHEST, preferred_element_type=F32)
    latent_bias = latent_bias[:1] + jnp.concatenate([mb_ref[...]] * 8, 1)
    aux_ref[...] = jnp.broadcast_to(latent_bias, aux_ref.shape)
    w_ref[...] = ((w.astype(F32) - mean_col) * gain).astype(BF)


BLOCKS = 10


def embed_kernel(arrived_ref, base_ref, w_ref, vec_ref, gram_ref, aux_ref, cross_ref, out_hbm, out_ref, sem):
    block = w_ref.shape[1] // BLOCKS
    columns = lambda n: pl.ds(n * block, block)
    tokens = base_ref.shape[0]
    lanes = arrived_ref.shape[1]
    z = lanes // 8
    both = arrived_ref[:tokens].astype(F32) + arrived_ref[tokens:].astype(F32)
    crossed = pltpu.roll(both, lanes // 2, 1)
    row = iota((tokens, 1), 0)
    down = jnp.where(row == 0, 0.0, pltpu.roll(crossed, 1, 0))
    up = jnp.where(row == tokens - 1, 0.0, pltpu.roll(crossed, tokens - 1, 0))
    lane = iota((1, lanes), 1)
    latent = both + jnp.where(lane // z % 2 == 0, down, up) + aux_ref[0:1]
    front = jnp.where(lane < lanes // 2, latent, base_ref[:, :lanes].astype(F32))
    x = jnp.concatenate([front.astype(BF), base_ref[:, lanes:]], 1)
    one = jnp.where(lane == lanes // 2, 1.0, 0.0)
    own = jnp.where(lane < lanes // 2, latent.astype(BF).astype(F32), one)
    y = dot(jnp.concatenate([own.astype(BF)] * 2, 1), gram_ref[...]) + cross_ref[...]
    variance = jnp.sum(y * own, axis=1, keepdims=True)
    scale = lax.rsqrt(jnp.maximum(variance, 0.0) + 1e-6)
    sent = []
    for n in range(BLOCKS):
        at = slice(n * block, (n + 1) * block)
        centred = dot(x, w_ref[:, at]) + vec_ref[0:1, at]
        out_ref[:, at] = (centred * scale + vec_ref[1:2, at]).astype(BF)
        copy = pltpu.make_async_copy(out_ref.at[:, columns(n)], out_hbm.at[:, columns(n)], sem.at[n])
        copy.start()
        sent.append(copy)
    for copy in sent:
        copy.wait()


def body(
    section_input, norm_gain, conv_weight, conv_bias, mean_weight, mean_bias, noisy_tokens, mask_tokens,
    patch_weight, patch_bias, context_weight, context_bias, norm_shift, norm_scale,
):
    frames, height, columns, channels = section_input.shape
    z = mean_weight.shape[1]
    tokens = noisy_tokens.shape[0]
    width = patch_weight.shape[1]
    features = patch_weight.shape[0] + context_weight.shape[0]
    shards = lax.axis_size("tile") * lax.axis_size("seq")
    tile = lax.axis_index("tile").astype(jnp.int32).reshape(1)
    vmem = pl.BlockSpec(memory_space=pltpu.VMEM)
    hbm = pl.BlockSpec(memory_space=pltpu.HBM)
    params = lambda mib: pltpu.CompilerParams(vmem_limit_bytes=mib * 1024 * 1024)
    row = lambda v: v.reshape(1, -1)
    taps_out = conv_weight.shape[1]
    dma = pltpu.SemaphoreType.DMA
    message = pl.pallas_call(
        encode_kernel,
        out_shape=jax.ShapeDtypeStruct((shards * 4, 8 * z), BF),
        in_specs=[pl.BlockSpec(memory_space=pltpu.SMEM)] + [hbm] * 4,
        out_specs=vmem,
        scratch_shapes=[
            pltpu.VMEM(section_input.shape, BF),
            pltpu.VMEM(norm_gain.shape, F32),
            pltpu.VMEM((taps_out, channels), BF),
            pltpu.VMEM(mean_weight.shape[::-1], F32),
            pltpu.VMEM((height // 2 + 1, frames * columns, 2 * channels), BF),
            pltpu.VMEM((2 * 8 * z, 4 * channels), BF),
            pltpu.VMEM((2 * 8 * z, 2 * channels), BF),
            pltpu.VMEM((shards * 8, 8 * z), F32),
            dma((3 + height // 2 // STEP,)),
        ],
        compiler_params=params(24),
        name="encode",
    )(tile, *in_hbm(section_input, norm_gain, conv_weight.T, mean_weight.T))
    arrived = lax.all_to_all(message.reshape(shards, 4, 8 * z), ("tile", "seq"), 0, 0)
    arrived = arrived.reshape(shards * 4, 8 * z)
    weights, vectors, gram, aux, base, cross = pl.pallas_call(
        prep_kernel,
        out_shape=(
            jax.ShapeDtypeStruct((features, width), BF),
            jax.ShapeDtypeStruct((2, width), F32),
            jax.ShapeDtypeStruct((16 * z, 8 * z), BF),
            jax.ShapeDtypeStruct((8, 8 * z), F32),
            jax.ShapeDtypeStruct((tokens, features), BF),
            jax.ShapeDtypeStruct((tokens, 8 * z), F32),
        ),
        in_specs=[hbm] * 11,
        out_specs=(vmem,) * 6,
        scratch_shapes=[
            pltpu.VMEM(mask_tokens.shape, BF),
            pltpu.VMEM((4 * z, width), BF),
            pltpu.VMEM((4, 1, width), F32),
            pltpu.VMEM(noisy_tokens.shape[::-1], BF),
            pltpu.VMEM((1, conv_bias.shape[0]), F32),
            pltpu.VMEM(mean_weight.shape[::-1], F32),
            pltpu.VMEM((1, z), F32),
            dma((12,)),
        ],
        compiler_params=params(24),
        cost_estimate=pl.CostEstimate(flops=2 * features * features * width, bytes_accessed=6_000_000, transcendentals=0),
        name="prep",
    )(
        *in_hbm(
            context_weight, patch_weight, row(patch_bias), row(context_bias), row(norm_shift), row(norm_scale),
            noisy_tokens.T, mask_tokens, row(conv_bias), mean_weight.T, row(mean_bias),
        )
    )
    return pl.pallas_call(
        embed_kernel,
        out_shape=jax.ShapeDtypeStruct((tokens, width), BF),
        in_specs=[vmem] * 7,
        out_specs=hbm,
        scratch_shapes=[
            pltpu.VMEM((tokens, width), BF),
            dma((BLOCKS,)),
        ],
        compiler_params=params(24),
        name="embed",
    )(*in_vmem(arrived, base, weights, vectors, gram, aux, cross))


def solution(mesh):
    placed = (
        P("tile", None, "seq", None),
        P(),
        P(),
        P(),
        P(),
        P(),
        P(("seq", "tile"), None),
        P(("seq", "tile"), None),
        P(),
        P(),
        P(),
        P(),
        P(),
        P(),
    )
    return jax.shard_map(
        body, mesh=mesh, in_specs=placed, out_specs=P(("seq", "tile"), None), check_vma=False
    )
```

```python
import jax
import jax.numpy as jnp
from jax import lax
from jax.experimental import pallas as pl
from jax.experimental.pallas import tpu as pltpu
from jax.sharding import PartitionSpec as P

BF = jnp.bfloat16
F32 = jnp.float32
NT = (((1,), (1,)), ((), ()))


def iota(shape, dim):
    return lax.broadcasted_iota(jnp.int32, shape, dim)


def dot(a, b):
    return jnp.dot(a, b, preferred_element_type=F32)


def dot_nt(a, b):
    return lax.dot_general(a, b, NT, preferred_element_type=F32)


def halves(x):
    high = x.astype(BF)
    return high, (x - high.astype(F32)).astype(BF)


SLOTS = ((0, 2), (0, 1), (1, 2), (1, 1), (0, 0), (0, 2), (1, 0), (1, 2))


def in_hbm(*arrays):
    return [pltpu.with_memory_space_constraint(x, pltpu.HBM) for x in arrays]


def in_vmem(*arrays):
    return [pltpu.with_memory_space_constraint(x, pltpu.VMEM) for x in arrays]


def fetch(sem, pairs):
    copies = [pltpu.make_async_copy(src, dst, sem.at[n]) for n, (src, dst) in enumerate(pairs)]
    for copy in copies:
        copy.start()
    return copies


STEP = 8
CHUNK = 32


def encode_kernel(tile_ref, x_hbm, gain_hbm, wt_hbm, mwt_hbm, out_ref, x_ref, gain_ref, wt_ref, mwt_ref, act, big, side, parts, sem):
    frames, height, columns, channels = x_ref.shape
    pairs = height // 2
    rows = frames * columns
    z, o = mwt_ref.shape
    taps = wt_ref.shape[0] // o
    span = lambda ref, n: ref.at[:, pl.ds(n * 2 * STEP, 2 * STEP)]
    blocks = pairs // STEP
    copies = fetch(
        sem,
        [(mwt_hbm, mwt_ref), (wt_hbm, wt_ref), (gain_hbm, gain_ref)]
        + [(span(x_hbm, n), span(x_ref, n)) for n in range(blocks)],
    )
    for copy in copies[: 3 + 2]:
        copy.wait()
    group = 4
    pick = (iota((o, group * o), 1) % o == iota((o, group * o), 0)).astype(BF)
    own = iota((group * z, group * o), 0) // z == iota((group * z, group * o), 1) // o
    spread = [jnp.where(own, jnp.concatenate([dot(part, pick)] * group, 0), 0.0) for part in halves(mwt_ref[...])]
    spread = jnp.concatenate(spread, 0).astype(BF)
    folded = []
    for tap in range(0, taps, group):
        count = min(group, taps - tap)
        term = dot(spread[:, : count * o], wt_ref[tap * o : (tap + count) * o])
        folded.append((term[: count * z] + term[group * z : (group + count) * z]).astype(BF))
    folded = jnp.concatenate(folded, 0)
    nothing = jnp.zeros((z, channels), BF)
    lanes = 8 * z
    for t in range(3):
        for slot, (a, e) in enumerate(SLOTS):
            at = (t * 8 + slot) * z
            for k in range(4):
                b = k - a
                tap = ((t * 3 + b) * 3 + e) * z
                value = folded[tap : tap + z] if 0 <= b < 3 else nothing
                if t:
                    big[at - lanes : at - lanes + z, k * channels : (k + 1) * channels] = value
                else:
                    row = at + k // 2 * lanes
                    side[row : row + z, k % 2 * channels : (k % 2 + 1) * channels] = value

    zero = jnp.zeros((rows, channels), BF)
    act[0, :, :channels] = zero
    act[pairs, :, channels:] = zero
    gain = 0.5 * gain_ref[...].reshape(1, 1, 1, channels)
    first = tile_ref[0] == 0
    def activate(j):
        x = x_ref[:, pl.ds(j * 2 * STEP, 2 * STEP)].astype(F32)
        energy = jnp.mean(x * x, axis=-1, keepdims=True)
        u = x * lax.rsqrt(energy + 1e-6) * gain
        v = u + u * jnp.tanh(u)
        v = jnp.concatenate([v[f] for f in range(frames)], axis=1).astype(BF)
        v = v.reshape(STEP, 2, rows, channels)
        act[pl.ds(j * STEP, STEP), :, channels:] = v[:, 0]
        act[pl.ds(j * STEP + 1, STEP), :, :channels] = v[:, 1]

    def convolve(c):
        both = act[c * CHUNK : (c + 1) * CHUNK + 1].reshape((CHUNK + 1) * rows, 2 * channels)
        low, high = both[:-rows], both[rows:]
        later = dot_nt(low, big[:, : 2 * channels]) + dot_nt(high, big[:, 2 * channels :])
        now = dot_nt(both, side[...])
        outs = (now[:-rows, :lanes] + now[rows:, lanes:], later[:, :lanes], later[:, lanes:])
        outs = [out.reshape(CHUNK // 2, 2, frames, columns, lanes) for out in outs]
        part = lambda p, f, t: outs[t][:, p, f]
        for p in range(2):
            ext = (
                part(p, 0, 2),
                part(p, 0, 1) + part(p, 1, 2),
                part(p, 0, 0) + part(p, 1, 1),
                part(p, 1, 0),
            )
            slots = (
                jnp.where(first, ext[0], 0.0),
                jnp.where(first, ext[1], 0.0),
                jnp.where(first, ext[2], ext[0]),
                jnp.where(first, ext[3], ext[1]),
            )
            for f in range(4):
                for m in range(CHUNK // 2):
                    at = (f * pairs + c * CHUNK + 2 * m + p) * columns
                    parts[at : at + columns] = slots[f][m]

    done = 0
    for j in range(blocks):
        if j == 2:
            for copy in copies[3 + 2 :]:
                copy.wait()
        activate(j)
        while (done + 1) * CHUNK + 1 <= (j + 1) * STEP:
            convolve(done)
            done += 1
    while done * CHUNK < pairs:
        convolve(done)
        done += 1

    total = parts.shape[0]
    even = parts[pl.ds(0, total // 2, stride=2)]
    odd = parts[pl.ds(1, total // 2, stride=2)]
    slot = iota((1, lanes), 1) // z
    near = pltpu.roll(even, lanes - z, 1)
    far = pltpu.roll(even, lanes - 3 * z, 1)
    moved = jnp.where((slot == 0) | (slot == 2), near, jnp.where((slot == 1) | (slot == 3), far, 0.0))
    back = (slot == 5) | (slot == 7)
    out_ref[...] = jnp.where(back, even, moved + odd).astype(BF)


def prep_kernel(
    ctx_hbm, patch_hbm, pb_hbm, cb_hbm, shift_hbm, scale_hbm, noisy_hbm, mask_hbm, conv_bias_hbm, mwt_hbm, mb_hbm,
    w_ref, vec_ref, gram_ref, aux_ref, base_ref, cross_ref,
    mask_ref, ctx_ref, rows_ref, noisy_ref, conv_bias_ref, mwt_ref, mb_ref, sem,
):
    z = mwt_ref.shape[0]
    lat = 4 * z
    width = w_ref.shape[1]
    size = w_ref.shape[0]
    copies = fetch(
        sem,
        [
            (ctx_hbm.at[pl.ds(0, lat)], ctx_ref),
            (patch_hbm, w_ref.at[pl.ds(lat, lat)]),
            (ctx_hbm.at[pl.ds(lat, 2 * lat)], w_ref.at[pl.ds(2 * lat, 2 * lat)]),
            (pb_hbm, rows_ref.at[0]),
            (cb_hbm, rows_ref.at[1]),
            (shift_hbm, rows_ref.at[2]),
            (scale_hbm, rows_ref.at[3]),
            (noisy_hbm, noisy_ref),
            (mask_hbm, mask_ref),
            (conv_bias_hbm, conv_bias_ref),
            (mwt_hbm, mwt_ref),
            (mb_hbm, mb_ref),
        ],
    )
    for copy in copies:
        copy.wait()
    row, col = iota((lat, lat), 0), iota((lat, lat), 1)
    order = (col == (row % z) * 4 + row // z).astype(BF)
    w_ref[:lat] = dot(order, ctx_ref[...]).astype(BF)
    bias = rows_ref[0] + rows_ref[1]
    mean_b = jnp.mean(bias, axis=1, keepdims=True)
    centred = bias - mean_b
    gain = 1.0 + rows_ref[3]
    vec_ref[0:1] = centred * gain
    vec_ref[1:2] = rows_ref[2]
    w = w_ref[...]
    high, low = halves(centred)
    rows = jnp.concatenate([jnp.ones((1, width), BF), high, low, jnp.zeros((5, width), BF)], 0)
    sums = dot_nt(rows, w)
    mean_w = sums[0:1] / width
    ones = jnp.ones((128, width), BF)
    mean_col = dot_nt(w, ones)[:, :1] / width
    gram = dot_nt(w, w) / width - mean_col * mean_w
    high, low = halves(gram)
    half = 2 * lat
    inside = (iota((half, half), 0) < lat) & (iota((half, half), 1) < lat)
    nil = jnp.zeros((half, half), BF)
    gram_ref[:half] = jnp.where(inside, high[:half, :half], nil)
    gram_ref[half:] = jnp.where(inside, low[:half, :half], nil)
    place = (iota((lat, half), 1) == iota((lat, half), 0) + lat).astype(BF)
    noisy = lax.dot_general(noisy_ref[...], place, (((0,), (0,)), ((), ())), preferred_element_type=F32).astype(BF)
    base_ref[:, :half] = noisy
    local = jnp.concatenate([noisy, mask_ref[...]], 1)
    base_ref[:, half:] = mask_ref[...]
    linear = 2.0 * (sums[1:2] + sums[2:3]) / width
    square = jnp.mean(centred * centred, axis=1, keepdims=True)
    tokens = local.shape[0]
    for r in range(0, tokens, tokens // 2):
        part = local[r : r + tokens // 2]
        y = dot(part, high) + dot(part, low)
        alone = jnp.sum((y + linear) * part.astype(F32), axis=1, keepdims=True) + square
        lane = iota((1, half), 1)
        cross_ref[r : r + tokens // 2] = jnp.where(
            lane < lat, 2.0 * y[:, :half] + linear[:, :half], jnp.where(lane == lat, alone, 0.0)
        )
    tiled = jnp.concatenate([mwt_ref[...]] * 8, 0)
    conv_bias = jnp.broadcast_to(conv_bias_ref[...], (8, conv_bias_ref.shape[1]))
    latent_bias = lax.dot_general(conv_bias, tiled, NT, precision=lax.Precision.HIGHEST, preferred_element_type=F32)
    latent_bias = latent_bias[:1] + jnp.concatenate([mb_ref[...]] * 8, 1)
    aux_ref[...] = jnp.broadcast_to(latent_bias, aux_ref.shape)
    w_ref[...] = ((w.astype(F32) - mean_col) * gain).astype(BF)


BLOCKS = 10


def embed_kernel(arrived_ref, base_ref, w_ref, vec_ref, gram_ref, aux_ref, cross_ref, out_hbm, out_ref, sem):
    block = w_ref.shape[1] // BLOCKS
    columns = lambda n: pl.ds(n * block, block)
    tokens = base_ref.shape[0]
    lanes = arrived_ref.shape[1]
    z = lanes // 8
    arrived = arrived_ref[...].astype(F32).reshape(tokens // 4, 8, lanes)
    both = (arrived[:, :4] + arrived[:, 4:]).reshape(tokens, lanes)
    crossed = pltpu.roll(both, lanes // 2, 1)
    row = iota((tokens, 1), 0)
    down = jnp.where(row == 0, 0.0, pltpu.roll(crossed, 1, 0))
    up = jnp.where(row == tokens - 1, 0.0, pltpu.roll(crossed, tokens - 1, 0))
    lane = iota((1, lanes), 1)
    latent = both + jnp.where(lane // z % 2 == 0, down, up) + aux_ref[0:1]
    front = jnp.where(lane < lanes // 2, latent, base_ref[:, :lanes].astype(F32))
    x = jnp.concatenate([front.astype(BF), base_ref[:, lanes:]], 1)
    one = jnp.where(lane == lanes // 2, 1.0, 0.0)
    own = jnp.where(lane < lanes // 2, latent.astype(BF).astype(F32), one)
    y = dot(jnp.concatenate([own.astype(BF)] * 2, 1), gram_ref[...]) + cross_ref[...]
    variance = jnp.sum(y * own, axis=1, keepdims=True)
    scale = lax.rsqrt(jnp.maximum(variance, 0.0) + 1e-6)
    sent = []
    for n in range(BLOCKS):
        at = slice(n * block, (n + 1) * block)
        centred = dot(x, w_ref[:, at]) + vec_ref[0:1, at]
        out_ref[:, at] = (centred * scale + vec_ref[1:2, at]).astype(BF)
        copy = pltpu.make_async_copy(out_ref.at[:, columns(n)], out_hbm.at[:, columns(n)], sem.at[n])
        copy.start()
        sent.append(copy)
    for copy in sent:
        copy.wait()


def body(
    section_input, norm_gain, conv_weight, conv_bias, mean_weight, mean_bias, noisy_tokens, mask_tokens,
    patch_weight, patch_bias, context_weight, context_bias, norm_shift, norm_scale,
):
    frames, height, columns, channels = section_input.shape
    z = mean_weight.shape[1]
    tokens = noisy_tokens.shape[0]
    width = patch_weight.shape[1]
    features = patch_weight.shape[0] + context_weight.shape[0]
    shards = lax.axis_size("tile") * lax.axis_size("seq")
    tile = lax.axis_index("tile").astype(jnp.int32).reshape(1)
    vmem = pl.BlockSpec(memory_space=pltpu.VMEM)
    hbm = pl.BlockSpec(memory_space=pltpu.HBM)
    params = lambda mib: pltpu.CompilerParams(vmem_limit_bytes=mib * 1024 * 1024)
    row = lambda v: v.reshape(1, -1)
    taps_out = conv_weight.shape[1]
    dma = pltpu.SemaphoreType.DMA
    message = pl.pallas_call(
        encode_kernel,
        out_shape=jax.ShapeDtypeStruct((shards * 4, 8 * z), BF),
        in_specs=[pl.BlockSpec(memory_space=pltpu.SMEM)] + [hbm] * 4,
        out_specs=vmem,
        scratch_shapes=[
            pltpu.VMEM(section_input.shape, BF),
            pltpu.VMEM(norm_gain.shape, F32),
            pltpu.VMEM((taps_out, channels), BF),
            pltpu.VMEM(mean_weight.shape[::-1], F32),
            pltpu.VMEM((height // 2 + 1, frames * columns, 2 * channels), BF),
            pltpu.VMEM((2 * 8 * z, 4 * channels), BF),
            pltpu.VMEM((2 * 8 * z, 2 * channels), BF),
            pltpu.VMEM((shards * 8, 8 * z), F32),
            dma((3 + height // 2 // STEP,)),
        ],
        compiler_params=params(24),
        name="encode",
    )(tile, *in_hbm(section_input, norm_gain, conv_weight.T, mean_weight.T))
    arrived = lax.all_to_all(message.reshape(shards, 4, 8 * z), ("seq", "tile"), 0, 0)
    arrived = arrived.reshape(shards * 4, 8 * z)
    weights, vectors, gram, aux, base, cross = pl.pallas_call(
        prep_kernel,
        out_shape=(
            jax.ShapeDtypeStruct((features, width), BF),
            jax.ShapeDtypeStruct((2, width), F32),
            jax.ShapeDtypeStruct((16 * z, 8 * z), BF),
            jax.ShapeDtypeStruct((8, 8 * z), F32),
            jax.ShapeDtypeStruct((tokens, features), BF),
            jax.ShapeDtypeStruct((tokens, 8 * z), F32),
        ),
        in_specs=[hbm] * 11,
        out_specs=(vmem,) * 6,
        scratch_shapes=[
            pltpu.VMEM(mask_tokens.shape, BF),
            pltpu.VMEM((4 * z, width), BF),
            pltpu.VMEM((4, 1, width), F32),
            pltpu.VMEM(noisy_tokens.shape[::-1], BF),
            pltpu.VMEM((1, conv_bias.shape[0]), F32),
            pltpu.VMEM(mean_weight.shape[::-1], F32),
            pltpu.VMEM((1, z), F32),
            dma((12,)),
        ],
        compiler_params=params(24),
        cost_estimate=pl.CostEstimate(flops=2 * features * features * width, bytes_accessed=6_000_000, transcendentals=0),
        name="prep",
    )(
        *in_hbm(
            context_weight, patch_weight, row(patch_bias), row(context_bias), row(norm_shift), row(norm_scale),
            noisy_tokens.T, mask_tokens, row(conv_bias), mean_weight.T, row(mean_bias),
        )
    )
    return pl.pallas_call(
        embed_kernel,
        out_shape=jax.ShapeDtypeStruct((tokens, width), BF),
        in_specs=[vmem] * 7,
        out_specs=hbm,
        scratch_shapes=[
            pltpu.VMEM((tokens, width), BF),
            dma((BLOCKS,)),
        ],
        compiler_params=params(24),
        name="embed",
    )(*in_vmem(arrived, base, weights, vectors, gram, aux, cross))


def solution(mesh):
    placed = (
        P("tile", None, "seq", None),
        P(),
        P(),
        P(),
        P(),
        P(),
        P(("seq", "tile"), None),
        P(("seq", "tile"), None),
        P(),
        P(),
        P(),
        P(),
        P(),
        P(),
    )
    return jax.shard_map(
        body, mesh=mesh, in_specs=placed, out_specs=P(("seq", "tile"), None), check_vma=False
    )
```
